512 devices in a mesh: ctx: 16 (over x, y), exp: 32 (over z, core).
Axes of the slice: x: 4, y: 4, z: 16, core: 2. Of those that a mesh axis runs over, the one named last changes fastest.
Arguments:
- query_matrix_rows: bfloat16 [16384, 4096], P('ctx', 'exp'), may hold values from -6 to 6
- key_matrix_rows: bfloat16 [16384, 4096], P('ctx', 'exp'), may hold values from -6 to 6
- value_matrix_rows: bfloat16 [16384, 4096], P('ctx', 'exp'), may hold values from -6 to 6
- strength: float32 [32, 16384], P('exp', 'ctx'), may hold values from 0.00390625 to 0.0234375
- channel_forget_rate: float32 [32, 128], P('exp'), may hold values from 3.0517578e-06 to 0.03125
- forget_rate_factor: float32 [32, 16384], P('exp', 'ctx'), may hold values from 0.5 to 2
- extra_log_decay: float32 [32, 16384], P('exp', 'ctx'), may hold values from 0 to 0.69
- initial_head_state: float32 [32, 128, 128], P('exp'), may hold values from -4 to 4
- other_residual_input: bfloat16 [65536, 1152], P(('ctx', 'exp')), may hold values from -75 to 75
- token_segment_index: int32 [65536], P(('ctx', 'exp')), may hold values from 0 to 2047, never falling along the last dimension, each value on 1 to 128 neighbouring positions
- routes: int32 [65536, 8], P(('ctx', 'exp')), may hold values from 0 to 31, all different within a row; in each aligned block of 128 rows (0 to 127, 128 to 255, ...) at most 40 rows name the same one
- modality_norm_gain: float32 [3, 1152], replicated, may hold values from 0.1 to 1.9
- router_projection_weight: bfloat16 [1152, 32], replicated, may hold values from -0.1875 to 0.1875
- expert_gate_weight: bfloat16 [32, 1152, 512], P('exp', 'ctx'), may hold values from -0.1875 to 0.1875
- expert_up_weight: bfloat16 [32, 1152, 512], P('exp', 'ctx'), may hold values from -0.1875 to 0.1875
- expert_down_weight: bfloat16 [32, 512, 1152], P('exp', 'ctx'), may hold values from -0.25 to 0.25
Outputs:
- delta_attention_output: bfloat16 [16384, 4096], P('ctx', 'exp')
- context_group_state: float32 [16, 32, 128, 128], P('ctx', 'exp')
- mixer_out: bfloat16 [65536, 1152], P(('ctx', 'exp'))
The draws below stay inside these ranges and needn't reach their ends.
Inputs may be any that keep to these rules, and one draw needn't show every extreme that they name: `routes`: in each aligned block of 128 rows (the rows of one device) no expert is named by more than 40 rows, a bound that some block reaches. A row names 8 different experts. `token_segment_index`: never falling along the tokens.
All inputs are finite; a program needn't handle non-finite values.
Results may differ from the reference program's by a relative error of at most 0.0077.
Values may be sent and summed in bfloat16 or wider, within the bound.
A program may use at most 64 MiB of HBM per device.

```python
import math
import jax
import jax.numpy as jnp
import numpy as np
from jax import lax

D = 1152
FE = 512
HEADS = 32
HD = 128
EXPERTS = 32
TOP = 8
MODAL = 3
STRIDE_POSITIONS = 256
ATT_TOK = 1024
TOK_DEV = 128
CAP = 40
ATT_TOKENS = 16384
TOKENS_MOE = 65536
SEGS = 2048


def draw_channel_forget_rate(key, part):
    key = jax.random.fold_in(key, 11)
    chooser_key, fast_key, slow_key = jax.random.split(key, 3)
    slow_share = 0.5
    chooser = jax.random.uniform(chooser_key, (HEADS, HD))
    fast_rate = jnp.exp(jax.random.uniform(fast_key, (HEADS, HD), minval=math.log(5.0), maxval=math.log(8.0))) / STRIDE_POSITIONS
    slow_rate = jnp.exp(jax.random.uniform(slow_key, (HEADS, HD), minval=math.log(0.05), maxval=math.log(0.5))) / ATT_TOKENS
    return jnp.where(chooser < slow_share, slow_rate, fast_rate).astype(jnp.float32)


def draw_extra_log_decay(key, part):
    key = jax.random.fold_in(key, 12)
    where_key, amount_key = jax.random.split(key, 2)
    struck = jax.random.uniform(where_key, (HEADS, ATT_TOKENS)) < 6.0 / ATT_TOKENS
    amount = jax.random.uniform(amount_key, (HEADS, ATT_TOKENS), minval=0.22, maxval=0.69)
    return jnp.where(struck, amount, 0.0).astype(jnp.float32)


def draw_other_residual_input(key, part):
    key = jax.random.fold_in(key, 13)
    column_key, row_key, under_key = jax.random.split(key, 3)
    column_scale = jnp.exp(jax.random.uniform(column_key, (1, D), maxval=math.log(10.0)))
    row_scale = jnp.exp(jax.random.uniform(row_key, (TOKENS_MOE, 1), maxval=math.log(10.0)))
    underlying = jnp.clip(jax.random.normal(under_key, (TOKENS_MOE, D)), -5.0, 5.0)
    return (0.15 * underlying * column_scale * row_scale).astype(jnp.bfloat16)


def levels(key, shape, cuts, smallest, largest):
    def one(axis_at, shards_of):
        draws = jax.random.uniform(jax.random.fold_in(jax.random.fold_in(key, 6), axis_at), (shards_of,), jnp.float32, smallest / len(cuts), largest / len(cuts))
        return jnp.repeat(jnp.exp(draws), shape[axis_at] // shards_of).reshape((-1,) + (1,) * (len(shape) - axis_at - 1))

    factor_of = one(*cuts[0])
    for cut in cuts[1:]:
        factor_of = factor_of * one(*cut)
    return factor_of


def split_up(number_of, total, bound, slope):
    weights = [(1 << 20) // math.isqrt(rank ** slope) + 1 for rank in range(2, number_of + 1)]
    surplus, given = total - bound - (number_of - 1), [1] * (number_of - 1)
    while surplus > 0:
        free = [i for i in range(number_of - 1) if given[i] < bound]
        mass, remaining = sum([weights[i] for i in free]), surplus
        for i in free:
            more = min(bound - given[i], max(1, remaining * weights[i] // mass), surplus)
            given[i] = given[i] + more
            surplus = surplus - more
    return np.array([bound] + given)


def uneven(stream_key, count, total, most, slope):
    if count == 2:
        one = jax.random.randint(stream_key, (), max(1, total - most), min(most, total - 1) + 1)
        return jnp.stack([one, total - one])
    sizes = jnp.asarray(split_up(count, total, most, slope), jnp.int32)
    twos = (count - 1) // 2
    source_of, taker = sizes[1:1 + 2 * twos:2], sizes[2:2 + 2 * twos:2]
    room = jnp.minimum(source_of - 1, most - taker)
    moved = jax.random.randint(jax.random.fold_in(stream_key, 1), (twos,), 0, 1 << 20) % (room + 1)
    sizes = sizes.at[1:1 + 2 * twos:2].set(source_of - moved).at[2:2 + 2 * twos:2].set(taker + moved)
    return sizes[jax.random.permutation(jax.random.fold_in(stream_key, 2), count)]


def routed_block(own_key, own, number, rows, count, top, limit, lean):
    sequence = jax.random.permutation(own_key, count)
    heavy_load, usual = shares(count, rows * top, limit, lean, True), shares(count, rows * top, limit, lean, False)
    places = jnp.arange(count)

    def named(tallies, turn):
        used = int((tallies > 0).sum())
        fixed = max(1, used // 4)
        passed = fixed + (places - fixed + turn * (used - fixed)) % max(1, count - fixed)
        return jnp.zeros((count,), jnp.int32).at[sequence[jnp.where(places < fixed, places, passed)]].set(jnp.asarray(tallies, jnp.int32))

    tallies = jnp.where(number % 4 == 0, named(heavy_load, number // 4), named(usual, number - number // 4 - 1))
    mixed = jax.random.permutation(jax.random.fold_in(own, 3), count)
    source_of, receiver = mixed[0:count // 2 * 2:2], mixed[1:count // 2 * 2:2]
    room = jnp.minimum(tallies[source_of] - 1, limit - tallies[receiver]) // 2
    room = jnp.where((source_of == sequence[0]) | (receiver == sequence[0]) | (tallies[receiver] == 0), 0, jnp.maximum(room, 0))
    passed = jax.random.randint(jax.random.fold_in(own, 4), (count // 2,), 0, 1 << 20) % (room + 1)
    tallies = tallies.at[source_of].add(-passed).at[receiver].add(passed)
    members = jnp.searchsorted(jnp.cumsum(tallies), jnp.arange(rows * top), side="right").astype(jnp.int32)
    grid = members.reshape(top, rows).T
    grid = grid[jax.random.permutation(jax.random.fold_in(own, 1), rows)]
    turn = jax.random.randint(jax.random.fold_in(own, 2), (rows, 1), 0, top)
    return jnp.take_along_axis(grid, (jnp.arange(top)[None, :] + turn) % top, axis=1)


def shares(count, total, reach, skew, full):
    loads = [(1 << 20) // math.isqrt(rank ** skew) + 1 for rank in range(1, count + 1)]
    largest = reach if full else min(reach, max(-(-total // count), total * loads[0] // sum(loads)))
    least = 1 if total - largest >= count - 1 else 0
    holding, surplus = [largest] + [least] * (count - 1), total - largest - least * (count - 1)
    while surplus > 0:
        free = [i for i in range(1, count) if holding[i] < largest] or [i for i in range(1, count) if holding[i] < reach]
        whole, budget = sum([loads[i] for i in free]), surplus
        for i in free:
            more = min(reach - holding[i], max(1, budget * loads[i] // whole), surplus)
            holding[i] = holding[i] + more
            surplus = surplus - more
    return np.array(holding)


def bell_draw(own_key, dims, deviation, bound, shards=(), held_as=jnp.bfloat16):
    array = deviation * jax.random.normal(own_key, dims, jnp.float32)
    if shards:
        array = array * levels(own_key, dims, shards, -0.22, 0.18)
    return jnp.clip(array, -bound, bound).astype(held_as)


def setup_inputs(seed: int = 0) -> dict:
    arg_keys = jax.random.split(jax.random.key(seed), 17)
    query_matrix_rows = bell_draw(arg_keys[0], (ATT_TOKENS, HEADS * HD), 1.0, 6.0, ((0, 16), (1, 32)))
    key_matrix_rows = bell_draw(arg_keys[1], (ATT_TOKENS, HEADS * HD), 1.0, 6.0, ((0, 16), (1, 32)))
    value_matrix_rows = bell_draw(arg_keys[2], (ATT_TOKENS, HEADS * HD), 1.0, 6.0, ((0, 16), (1, 32)))
    strength = jnp.clip(jnp.exp(math.log(0.0234375) - 1.7917595 * jax.random.uniform(arg_keys[3], (HEADS, ATT_TOKENS), jnp.float32) ** levels(arg_keys[3], (HEADS, ATT_TOKENS), ((0, 32), (1, 16)), -0.2, 0.2)), 0.00390625, 0.0234375)
    channel_forget_rate = draw_channel_forget_rate(jax.random.fold_in(arg_keys[16], 71), 0)
    forget_rate_factor = jnp.clip(jnp.exp(math.log(2.0) - 1.3862944 * jax.random.uniform(arg_keys[5], (HEADS, ATT_TOKENS), jnp.float32) ** levels(arg_keys[5], (HEADS, ATT_TOKENS), ((0, 32), (1, 16)), -0.2, 0.2)), 0.5, 2.0)
    extra_log_decay = draw_extra_log_decay(jax.random.fold_in(arg_keys[16], 71), 0)
    initial_head_state = bell_draw(arg_keys[7], (HEADS, HD, HD), 0.3, 4.0, ((0, 32),), jnp.float32)
    other_residual_input = draw_other_residual_input(jax.random.fold_in(arg_keys[16], 71), 0)
    token_segment_index = jnp.searchsorted(jnp.cumsum(uneven(arg_keys[9], SEGS, TOKENS_MOE, TOK_DEV, 1)), jnp.arange(TOKENS_MOE), side="right").astype(jnp.int32)
    routes_keys = jax.random.split(jax.random.fold_in(arg_keys[10], 1), TOKENS_MOE // TOK_DEV)
    routes_turns = jax.random.permutation(jax.random.fold_in(arg_keys[10], 3), TOKENS_MOE // TOK_DEV)
    routes = jax.vmap(lambda own, number: routed_block(jax.random.fold_in(arg_keys[10], 2), own, number, TOK_DEV, EXPERTS, TOP, CAP, 2))(routes_keys, routes_turns).reshape((TOKENS_MOE, TOP))
    modality_norm_gain = jnp.clip(1.0 + 0.18 * jax.random.normal(arg_keys[11], (MODAL, D), jnp.float32), 0.1, 1.9)
    router_projection_weight = bell_draw(arg_keys[12], (D, EXPERTS), D ** -0.5, 0.1875)
    expert_gate_weight = bell_draw(arg_keys[13], (EXPERTS, D, FE), D ** -0.5, 0.1875, ((0, 32), (1, 16)))
    expert_up_weight = bell_draw(arg_keys[14], (EXPERTS, D, FE), D ** -0.5, 0.1875, ((0, 32), (1, 16)))
    expert_down_weight = bell_draw(arg_keys[15], (EXPERTS, FE, D), FE ** -0.5, 0.25, ((0, 32), (1, 16)))
    return {"query_matrix_rows": query_matrix_rows, "key_matrix_rows": key_matrix_rows, "value_matrix_rows": value_matrix_rows, "strength": strength, "channel_forget_rate": channel_forget_rate, "forget_rate_factor": forget_rate_factor, "extra_log_decay": extra_log_decay, "initial_head_state": initial_head_state, "other_residual_input": other_residual_input, "token_segment_index": token_segment_index, "routes": routes, "modality_norm_gain": modality_norm_gain, "router_projection_weight": router_projection_weight, "expert_gate_weight": expert_gate_weight, "expert_up_weight": expert_up_weight, "expert_down_weight": expert_down_weight}


exact = lax.Precision.HIGHEST
route_scale = 2.446
norm_eps = 1e-06

def unit_rows(values):
    return values * lax.rsqrt(lax.optimization_barrier(jnp.sum(values * values, axis=-1, keepdims=True)) + norm_eps)

def span_terms(query_unit, key_unit, values, strengths, summed_fading_exponent):
    length = query_unit.shape[2]
    head_dim = values.shape[-1]
    cumulative = jnp.cumsum(summed_fading_exponent, axis=2)
    final_log = cumulative[:, :, length - 1:, :]
    key_grown = key_unit * jnp.exp(cumulative)
    key_shrunk = key_unit * jnp.exp(-cumulative)
    query_grown = query_unit * jnp.exp(cumulative)
    key_scores = jnp.einsum('hntc,hnsc->hnts', key_grown, key_shrunk, precision=exact)
    query_scores = jnp.einsum('hntc,hnsc->hnts', query_grown, key_shrunk, precision=exact)
    strict = jnp.tril(jnp.ones((length, length), jnp.float32), -1)
    inclusive = jnp.tril(jnp.ones((length, length), jnp.float32))
    system = jnp.eye(length, dtype=jnp.float32) + strengths[..., None] * key_scores * strict
    right_side = strengths[..., None] * jnp.concatenate([values, key_grown], axis=-1)
    solved = jax.scipy.linalg.solve_triangular(system, right_side, lower=True, unit_diagonal=True)
    written = solved[..., :head_dim]
    key_solved = solved[..., head_dim:]
    lower_scores = query_scores * inclusive
    inner_out = jnp.einsum('hnts,hnsd->hntd', lower_scores, written, precision=exact)
    reader = query_grown - jnp.einsum('hnts,hnsc->hntc', lower_scores, key_solved, precision=exact)
    key_end = key_unit * jnp.exp(final_log - cumulative)
    transition = jnp.exp(final_log)[:, :, 0, :, None] * jnp.eye(head_dim, dtype=jnp.float32)
    transition = transition - jnp.einsum('hnsc,hnsd->hncd', key_end, key_solved, precision=exact)
    addition = jnp.einsum('hnsc,hnsd->hncd', key_end, written, precision=exact)
    return (inner_out, reader, transition, addition)

def attention_portion(query_matrix_rows, key_matrix_rows, value_matrix_rows, strength, channel_forget_rate, forget_rate_factor, extra_log_decay, initial_head_state):
    stretch_bounds_array = ATT_TOKENS // STRIDE_POSITIONS
    per_group = ATT_TOK // STRIDE_POSITIONS

    def per_head_split(values):
        return values.reshape(ATT_TOKENS, HEADS, HD).transpose(1, 0, 2)

    def one_head(bundled_cluster):
        single_probe_piece, single_lookup_piece, single_payload_piece, single_beta_piece, single_fading_piece, single_learning_piece, single_surge_piece, starting_memory = bundled_cluster

        def shaped(values):
            return values.astype(jnp.float32).reshape(1, stretch_bounds_array, STRIDE_POSITIONS, HD)
        query_unit = unit_rows(shaped(single_probe_piece))
        key_unit = unit_rows(shaped(single_lookup_piece))
        values_now = shaped(single_payload_piece)
        strengths = single_beta_piece.reshape(1, stretch_bounds_array, STRIDE_POSITIONS)
        summed_fading_exponent = -(single_fading_piece[None, None, None, :] * single_learning_piece.reshape(1, stretch_bounds_array, STRIDE_POSITIONS, 1) + single_surge_piece.reshape(1, stretch_bounds_array, STRIDE_POSITIONS, 1))
        inner_out, reader, transition, addition = span_terms(query_unit, key_unit, values_now, strengths, summed_fading_exponent)

        def advance(current, pieces_now):
            inner_part, reader_part, trans_part, extra_part = pieces_now
            output_now = inner_part + jnp.einsum('htc,hcd->htd', reader_part, current, precision=exact)
            following = jnp.einsum('hce,hed->hcd', trans_part, current, precision=exact) + extra_part
            return (following, (output_now, following))
        pieces = tuple((jnp.moveaxis(item, 1, 0) for item in (inner_out, reader, transition, addition)))
        final_state, (outputs, states) = lax.scan(advance, starting_memory[None], pieces)
        return (outputs.reshape(ATT_TOKENS, HD), states[per_group - 1::per_group, 0])
    bundled_cluster = (per_head_split(query_matrix_rows), per_head_split(key_matrix_rows), per_head_split(value_matrix_rows), strength, channel_forget_rate, forget_rate_factor, extra_log_decay, initial_head_state)
    outputs, states = lax.map(one_head, bundled_cluster)
    delta_attention_output = outputs.transpose(1, 0, 2).reshape(ATT_TOKENS, HEADS * HD).astype(jnp.bfloat16)
    return (delta_attention_output, states.transpose(1, 0, 2, 3))

def mixer_part(other_residual_input, token_segment_index, routes, modality_norm_gain, router_projection_weight, expert_gate_weight, expert_up_weight, expert_down_weight):
    owners = TOKENS_MOE // TOK_DEV
    stream = other_residual_input.astype(jnp.float32)
    modality = token_segment_index % MODAL
    modal_pick = (modality[:, None] == jnp.arange(MODAL)[None, :]).astype(jnp.float32)
    gains = jnp.dot(modal_pick, modality_norm_gain, precision=exact)
    normed = (stream * lax.rsqrt(lax.optimization_barrier(jnp.mean(stream * stream, axis=1, keepdims=True)) + norm_eps) * gains).astype(jnp.bfloat16)
    logits = jnp.dot(normed.astype(jnp.float32), router_projection_weight.astype(jnp.float32), preferred_element_type=jnp.float32)
    picked = jnp.take_along_axis(logits, routes, axis=1)
    scores = jax.nn.sigmoid(picked)
    weights = (route_scale * scores / lax.optimization_barrier(jnp.sum(scores, axis=1, keepdims=True))).astype(jnp.bfloat16)
    chosen = routes[:, :, None] == jnp.arange(EXPERTS)[None, None, :]
    weight_table = lax.optimization_barrier(jnp.sum(jnp.where(chosen, weights.astype(jnp.float32)[:, :, None], 0.0), axis=1))
    weight_table = weight_table.reshape(owners, TOK_DEV, EXPERTS)
    hit_table = lax.optimization_barrier(jnp.sum(chosen.astype(jnp.int32), axis=1)).reshape(owners, TOK_DEV, EXPERTS)
    before_table = jnp.cumsum(hit_table, axis=1) - hit_table
    grouped = normed.reshape(owners, TOK_DEV, D)
    slot_ids = jnp.arange(CAP).astype(jnp.int32)
    token_ids = jnp.arange(TOK_DEV).astype(jnp.int32)

    def one_expert(accum, expert_index):
        hit_now = lax.dynamic_index_in_dim(hit_table, expert_index, axis=2, keepdims=False)
        slot_now = lax.dynamic_index_in_dim(before_table, expert_index, axis=2, keepdims=False)
        weight_now = lax.dynamic_index_in_dim(weight_table, expert_index, axis=2, keepdims=False)
        matched = (hit_now[:, :, None] == 1) & (slot_now[:, :, None] == slot_ids[None, None, :])
        index = lax.optimization_barrier(jnp.sum(jnp.where(matched, token_ids[None, :, None], 0), axis=1)).astype(jnp.int32)
        filled = jnp.any(matched, axis=1)
        rows_now = jnp.take_along_axis(grouped, index[:, :, None], axis=1)
        rows_now = jnp.where(filled[:, :, None], rows_now, jnp.zeros_like(rows_now)).reshape(owners * CAP, D)
        gate_acts = jnp.dot(rows_now.astype(jnp.float32), expert_gate_weight[expert_index].astype(jnp.float32), preferred_element_type=jnp.float32)
        up_acts = jnp.dot(rows_now.astype(jnp.float32), expert_up_weight[expert_index].astype(jnp.float32), preferred_element_type=jnp.float32)
        hidden = (jax.nn.silu(gate_acts) * up_acts).astype(jnp.bfloat16)
        produced = jnp.dot(hidden.astype(jnp.float32), expert_down_weight[expert_index].astype(jnp.float32), preferred_element_type=jnp.float32).astype(jnp.bfloat16)
        produced = produced.reshape(owners, CAP, D)
        slot_safe = jnp.clip(slot_now, 0, CAP - 1).astype(jnp.int32)
        fetched = jnp.take_along_axis(produced, slot_safe[:, :, None], axis=1).astype(jnp.float32)
        return (accum + fetched * weight_now[:, :, None], None)
    start = jnp.zeros((owners, TOK_DEV, D), jnp.float32)
    accum, unused = lax.scan(one_expert, start, jnp.arange(EXPERTS).astype(jnp.int32))
    return accum.reshape(TOKENS_MOE, D).astype(jnp.bfloat16)

def reference(query_matrix_rows, key_matrix_rows, value_matrix_rows, strength, channel_forget_rate, forget_rate_factor, extra_log_decay, initial_head_state, other_residual_input, token_segment_index, routes, modality_norm_gain, router_projection_weight, expert_gate_weight, expert_up_weight, expert_down_weight):
    delta_attention_output, context_group_state = attention_portion(query_matrix_rows, key_matrix_rows, value_matrix_rows, strength, channel_forget_rate, forget_rate_factor, extra_log_decay, initial_head_state)
    mixer_out = mixer_part(other_residual_input, token_segment_index, routes, modality_norm_gain, router_projection_weight, expert_gate_weight, expert_up_weight, expert_down_weight)
    return (delta_attention_output, context_group_state, mixer_out)
```

```python
import functools

import jax
import jax.numpy as jnp
from jax import lax
from jax.experimental import pallas as pl
from jax.experimental.pallas import tpu as pltpu
from jax.sharding import PartitionSpec as P

F32 = jnp.float32
BF = jnp.bfloat16
MESH = pl.DeviceIdType.MESH

C = 128
CHUNKS = 8
TOK = 128
CAP = 40
EXPERTS = 32
MODAL = 3
D = 1152
FE = 512
SIDE = 4
SHARDS = SIDE * SIDE
DEPTH = D // SHARDS
WIDTH = FE // SHARDS
WINDOW = 8
LOCAL = 4
route_scale = 2.446
norm_eps = 1e-06

SLOT = {4: 0, -3: 1, 3: 2, -2: 3, 2: 4, -1: 5, 1: 6, 0: 7}


def dn(a, b, ca, cb):
    return lax.dot_general(
        a.astype(BF), b.astype(BF), (((ca,), (cb,)), ((), ())), preferred_element_type=F32
    )


def split(a):
    high = a.astype(BF)
    return high, (a - high.astype(F32)).astype(BF)


def dot3(a, b):
    ah, al = split(a)
    bh, bl = split(b)
    return dn(ah, bh, 1, 0) + dn(ah, bl, 1, 0) + dn(al, bh, 1, 0)


def unit(v):
    return v * lax.rsqrt(jnp.sum(v * v, axis=-1, keepdims=True) + norm_eps)


def iotas(shape):
    return (
        lax.broadcasted_iota(jnp.int32, shape, 0),
        lax.broadcasted_iota(jnp.int32, shape, 1),
    )


def chunk_terms(n, q_ref, k_ref, v_ref, f_ref, x_ref, b_ref, rate_ref, readers, inner, added, decay):
    row, col = iotas((C, C))
    rows = pl.ds(pl.multiple_of(n * C, C), C)
    ku = unit(k_ref[rows, :].astype(F32))
    qu = unit(q_ref[rows, :].astype(F32))
    v = v_ref[rows, :].astype(F32)
    f = f_ref[pl.ds(n, 1), :]
    x = x_ref[pl.ds(n, 1), :]
    b = b_ref[pl.ds(n, 1), :]
    fc = jnp.sum(jnp.where(col <= row, f, 0.0), axis=1, keepdims=True)
    xc = jnp.sum(jnp.where(col <= row, x, 0.0), axis=1, keepdims=True)
    bc = jnp.sum(jnp.where(col == row, b, 0.0), axis=1, keepdims=True)
    cum = -(rate_ref[0:1, :] * fc + xc)
    last = cum[C - 1 : C, :]
    grown = jnp.exp(cum)
    kg = ku * grown
    ks = ku * jnp.exp(-cum)
    qg = qu * grown
    ke = ku * jnp.exp(last - cum)
    scores = dn(jnp.concatenate([kg, qg], 0), ks, 1, 1)
    a = jnp.where(col < row, scores[:C] * bc, 0.0)
    low = jnp.where(col <= row, scores[C:], 0.0)
    eye = jnp.where(col == row, 1.0, 0.0)
    inverse = eye - a
    square = dn(a, a, 1, 0)
    for level in range(6):
        if level < 5:
            r = dn(jnp.concatenate([inverse, square], 0), square, 1, 0)
            inverse = inverse + r[:C]
            square = r[C:]
        else:
            inverse = inverse + dn(inverse, square, 1, 0)
    solved = dn(inverse, jnp.concatenate([v * bc, kg * bc], 1), 1, 0)
    r1 = dn(low, solved, 1, 0)
    r2 = dn(ke, solved, 0, 0)
    inner[n] = r1[:, :C]
    readers[n] = jnp.concatenate([(qg - r1[:, C:]).astype(BF), r2[:, C:].astype(BF)], 0)
    added[n] = r2[:, :C]
    column = jnp.sum(jnp.where(col == row, jnp.exp(last), 0.0), axis=1, keepdims=True)
    decay[n] = jnp.broadcast_to(column, (C, C))


def kernel(
    q_ref, k_ref, v_ref, b_ref, rate_ref, f_ref, x_ref, s0_ref, res_ref, seg_ref, routes_ref,
    gain_ref, router_ref, gate_ref, up_ref, down_ref,
    att_ref, state_ref, mix_ref,
    gs, us, wg, wu, wd, relay_g, relay_d, tok, table, slot_ids, slot_w, xin, eo, contrib, rs_out,
    rs_in, readers, inner, added, decay, gmap, rowmaps, colmaps, state, send_sem, recv_sem, loc_sem,
):
    ctx = lax.axis_index("ctx")
    own = lax.axis_index("exp")
    px, py = ctx // SIDE, ctx % SIDE
    pz, core = own // 2, own % 2
    planes = EXPERTS // 2
    sense = 1 - 2 * core

    def along_z(steps):
        return (ctx, lax.rem(pz + sense * steps + planes, planes) * 2 + core)

    def along_x(steps):
        return (lax.rem(px + steps, SIDE) * SIDE + py, own)

    def along_y(steps):
        return (px * SIDE + lax.rem(py + steps, SIDE), own)

    sibling = (ctx, pz * 2 + 1 - core)
    ids = {}

    def remote(name, src, dst, device):
        k = ids.setdefault(name, len(ids))
        return pltpu.make_async_remote_copy(
            src_ref=src, dst_ref=dst, send_sem=send_sem.at[k], recv_sem=recv_sem.at[k],
            device_id=device, device_id_type=MESH,
        )

    started = []

    def go(copies):
        for one in copies:
            one.start()
        started.extend(copies)
        return copies

    def arrive(copies):
        for one in copies:
            one.wait_recv()

    shard_x = py * SIDE + px
    down_rows = pl.ds(pl.multiple_of(ctx * WIDTH, WIDTH), WIDTH)
    locals_ = [
        pltpu.make_async_copy(gate_ref.at[0], gs.at[0, shard_x], loc_sem.at[0]),
        pltpu.make_async_copy(up_ref.at[0], us.at[0, shard_x], loc_sem.at[1]),
        pltpu.make_async_copy(down_ref.at[0], wd.at[0, down_rows], loc_sem.at[2]),
    ]
    for one in locals_:
        one.start()

    barrier = pltpu.get_barrier_semaphore()
    partners = [along_z(t) for t in (1, -1, 4, -4)] + [sibling]
    partners += [along_x(t) for t in (1, 2, 3)] + [along_y(t) for t in (1, 2, 3)]
    for device in partners:
        pl.semaphore_signal(barrier, inc=1, device_id=device, device_id_type=MESH)
    pl.semaphore_wait(barrier, len(partners))

    hop1 = go([
        remote("bg1", gate_ref.at[0], relay_g.at[0], along_z(4)),
        remote("bu1", up_ref.at[0], relay_g.at[1], along_z(4)),
        remote("bd1", down_ref.at[0], relay_d, along_z(-4)),
    ])

    def first(r, g_src, u_src, d_src):
        copies = []
        for t in (1, 3, 2):
            copies.append(remote(f"g1{r}{t}", g_src, gs.at[r, shard_x], along_x(t)))
            if r == 0:
                copies.append(remote(f"u1{r}{t}", u_src, us.at[r, shard_x], along_x(t)))
            else:
                copies.append(remote(f"u1{r}{t}", u_src, us.at[r, ctx], along_y(t)))
            copies.append(remote(f"d1{r}{t}", d_src, wd.at[2 * r, down_rows], along_y(t)))
        return copies

    def second(r):
        copies = []
        by_x = pl.ds(py * SIDE, SIDE)
        by_y = pl.ds(px * SIDE, SIDE)
        block = pl.ds(pl.multiple_of(px * SIDE * WIDTH, SIDE * WIDTH), SIDE * WIDTH)
        for t in (1, 3, 2):
            copies.append(remote(f"g2{r}{t}", gs.at[r, by_x], gs.at[r, by_x], along_y(t)))
            if r == 0:
                copies.append(remote(f"u2{r}{t}", us.at[r, by_x], us.at[r, by_x], along_y(t)))
            else:
                copies.append(remote(f"u2{r}{t}", us.at[r, by_y], us.at[r, by_y], along_x(t)))
            copies.append(remote(f"d2{r}{t}", wd.at[2 * r, block], wd.at[2 * r, block], along_x(t)))
        return copies

    first_own = go(first(0, gate_ref.at[0], up_ref.at[0], down_ref.at[0]))

    row, col = iotas((C, C))
    stream = res_ref[...].astype(F32)
    scale = lax.rsqrt(jnp.mean(stream * stream, axis=1, keepdims=True) + norm_eps)
    seg = seg_ref[...].astype(F32)
    modality = seg - MODAL * jnp.floor((seg + 0.5) * (1.0 / MODAL))
    modality = jnp.sum(jnp.where(col == row, modality, 0.0), axis=1, keepdims=True)
    gains = jnp.where(
        modality == 0.0,
        gain_ref[0:1, :],
        jnp.where(modality == 1.0, gain_ref[1:2, :], gain_ref[2:3, :]),
    )
    normed = (stream * scale * gains).astype(BF)
    tok[SLOT[0]] = normed
    logits = dn(normed, router_ref[...], 1, 0)
    lane = lax.broadcasted_iota(jnp.int32, (TOK, EXPERTS), 1)
    hits = jnp.zeros((TOK, EXPERTS), F32)
    routes = routes_ref[...]
    for turn in range(8):
        hits = hits + jnp.where(routes[:, turn : turn + 1] == lane, 1.0, 0.0)
    scores = jnp.where(hits > 0.0, 1.0 / (1.0 + jnp.exp(-logits)), 0.0)
    weights = route_scale * scores / jnp.sum(scores, axis=1, keepdims=True)
    wide = jnp.concatenate([weights, jnp.zeros((TOK, C - EXPERTS), F32)], 1)
    table[SLOT[0]] = jnp.transpose(wide)[:EXPERTS].astype(BF)

    def token_step(way, k):
        near, far = SLOT[way * (k - 1)], SLOT[way * k]
        return [
            remote(f"t{way}{k}", tok.at[near], tok.at[far], along_z(way)),
            remote(f"w{way}{k}", table.at[near], table.at[far], along_z(way)),
        ]

    ahead = {1: go(token_step(1, 1))}
    behind = {1: go(token_step(-1, 1))}

    def pass_on(k):
        arrive(ahead[k])
        if k < 4:
            ahead[k + 1] = go(token_step(1, k + 1))
        if k <= 3:
            arrive(behind[k])
            if k < 3:
                behind[k + 1] = go(token_step(-1, k + 1))

    def chunks(lo, hi):
        def body(n, carry):
            chunk_terms(
                n, q_ref, k_ref, v_ref, f_ref, x_ref, b_ref, rate_ref, readers, inner, added, decay
            )
            return carry

        lax.fori_loop(lo, hi, body, 0)

    chunks(0, 2)
    arrive(hop1)
    here_g, here_u, here_d = gs.at[1, shard_x], us.at[1, ctx], wd.at[2, down_rows]
    hop2 = go([
        remote("bg2", relay_g.at[0], here_g, along_z(4)),
        remote("bu2", relay_g.at[1], here_u, along_z(4)),
        remote("bd2", relay_d, here_d, along_z(-4)),
    ])
    for one in locals_:
        one.wait()
    arrive(first_own)
    second_own = go(second(0))
    chunks(2, 4)
    pass_on(1)
    chunks(4, 6)
    arrive(hop2)
    first_far = go(first(1, here_g, here_u, here_d))
    chunks(6, 8)
    pass_on(2)

    gmap[...] = jnp.concatenate([jnp.zeros((C, C), F32), jnp.where(col == row, 1.0, 0.0)], 1)

    def grow(n, carry):
        d = decay[n]
        m = gmap[...]
        r = dn(readers[n, C:], m, 1, 0)
        gmap[...] = jnp.concatenate(
            [d * m[:, :C] - r[:, :C] + added[n], d * m[:, C:] - r[:, C:]], 1
        )
        return carry

    lax.fori_loop(0, CHUNKS, grow, 0)
    rowmaps[py] = gmap[...]
    row_copies = go([remote(f"r{t}", gmap, rowmaps.at[py], along_y(t)) for t in (1, 3, 2)])
    arrive(first_far)
    second_far = go(second(1))
    arrive(row_copies)
    whole = rowmaps[0]
    for t in range(1, SIDE):
        m = rowmaps[t]
        whole = dot3(m[:, C:], whole)
        whole = jnp.concatenate([whole[:, :C] + m[:, :C], whole[:, C:]], 1)
    colmaps[px] = whole
    col_copies = go([
        remote(f"c{t}", colmaps.at[px], colmaps.at[px], along_x(t)) for t in (1, 3, 2)
    ])
    pass_on(3)

    def merge(src, r, dst, x_first):
        def body(h, carry):
            parts = []
            for late in range(2):
                i = 2 * h + late
                place = (i % SIDE) * SIDE + i // SIDE if x_first else i
                parts.append(src[r, place].astype(F32))
            at = pl.ds(pl.multiple_of(h * 2 * DEPTH, 2 * DEPTH), 2 * DEPTH)
            dst[2 * r, at, :] = jnp.concatenate(parts, 0).astype(BF)
            return carry

        lax.fori_loop(0, SHARDS // 2, body, 0)

    def share(r):
        return go([
            remote(f"sg{r}", wg.at[2 * r], wg.at[2 * r + 1], sibling),
            remote(f"su{r}", wu.at[2 * r], wu.at[2 * r + 1], sibling),
            remote(f"sd{r}", wd.at[2 * r], wd.at[2 * r + 1], sibling),
        ])

    arrive(second_own)
    merge(gs, 0, wg, True)
    merge(us, 0, wu, True)
    share_own = share(0)
    arrive(col_copies)
    entering = s0_ref[0]
    for t in range(SIDE - 1):
        m = colmaps[t]
        entering = jnp.where(px > t, dot3(m[:, C:], entering) + m[:, :C], entering)
    for t in range(SIDE - 1):
        m = rowmaps[t]
        entering = jnp.where(py > t, dot3(m[:, C:], entering) + m[:, :C], entering)
    state[...] = entering

    def outputs(n, carry):
        s = state[...]
        r = dn(readers[n], s, 1, 0)
        att_ref[pl.ds(pl.multiple_of(n * C, C), C), :] = (inner[n] + r[:C]).astype(BF)
        state[...] = decay[n] * s - r[C:] + added[n]
        return carry

    lax.fori_loop(0, CHUNKS, outputs, 0)
    state_ref[0, 0] = state[...]
    pass_on(4)
    arrive(second_far)
    merge(gs, 1, wg, True)
    merge(us, 1, wu, False)
    share_far = share(1)

    upper = jnp.where(row <= col, 1.0, 0.0)
    pick_row, pick_col = iotas((8, EXPERTS))
    mine = []
    for r in range(2):
        plane = lax.rem(pz + 8 * r, planes)
        mine += [2 * plane + core, 2 * plane + 1 - core]
    select = jnp.zeros((8, EXPERTS), F32)
    for e in range(LOCAL):
        select = select + jnp.where((pick_row == e) & (pick_col == mine[e]), 1.0, 0.0)
    for slot in range(WINDOW):
        w = dn(select, table[slot], 1, 0)
        hit = w != 0.0
        place = dn(jnp.where(hit, 1.0, 0.0), upper, 1, 0)
        slot_ids[slot] = jnp.where(hit, place + (CAP * (slot % 2) - 1.0), -1.0)
        slot_w[slot] = w

    PAIR = 2 * CAP
    place_rows = lax.broadcasted_iota(jnp.int32, (PAIR, 2 * TOK), 0).astype(F32)

    def spread(pair, weighted):
        a, b = 2 * pair, 2 * pair + 1
        parts = []
        for e in range(LOCAL):
            ids_row = jnp.concatenate([slot_ids[a, e : e + 1, :], slot_ids[b, e : e + 1, :]], 1)
            if weighted:
                value = jnp.concatenate([slot_w[a, e : e + 1, :], slot_w[b, e : e + 1, :]], 1)
            else:
                value = 1.0
            parts.append(jnp.where(place_rows == ids_row, value, 0.0))
        return jnp.concatenate(parts, 0).astype(BF)

    def gather(group):
        for half in range(2):
            pair = 2 * group + half
            both = tok[2 * pair : 2 * pair + 2].reshape(2 * TOK, D)
            rows = dn(spread(pair, False), both, 1, 0).astype(BF)
            for e in range(LOCAL):
                xin[e, half * PAIR : (half + 1) * PAIR, :] = rows[e * PAIR : (e + 1) * PAIR]

    def experts():
        def body(e, carry):
            x = xin[e]
            g = dn(x, wg[e], 1, 0)
            u = dn(x, wu[e], 1, 0)
            hidden = (g / (1.0 + jnp.exp(-g)) * u).astype(BF)
            eo[e] = dn(hidden, wd[e], 1, 0).astype(BF)
            return carry

        lax.fori_loop(0, LOCAL, body, 0)

    def combine(group):
        for half in range(2):
            pair = 2 * group + half
            made = jnp.concatenate(
                [eo[e, half * PAIR : (half + 1) * PAIR, :] for e in range(LOCAL)], 0
            )
            both = dn(spread(pair, True), made, 0, 0)
            contrib[2 * pair] = both[:TOK].astype(BF)
            contrib[2 * pair + 1] = both[TOK:].astype(BF)

    gather(0)
    arrive(share_own)
    arrive(share_far)
    experts()
    combine(0)

    sums = {}

    def send_sum(distance):
        way = -1 if distance > 0 else 1
        at = SLOT[distance]
        last = 4 if distance > 0 else -3
        if distance == last:
            src = contrib.at[at]
        else:
            outer = sums[distance - way]
            arrive(outer)
            inbox = SLOT[distance - way]
            rs_out[at] = (contrib[at].astype(F32) + rs_in[inbox].astype(F32)).astype(BF)
            src = rs_out.at[at]
        sums[distance] = go([remote(f"s{distance}", src, rs_in.at[at], along_z(way))])

    send_sum(4)
    send_sum(-3)
    gather(1)
    experts()
    combine(1)
    send_sum(3)
    send_sum(-2)
    send_sum(2)
    send_sum(-1)
    send_sum(1)
    arrive(sums[-1])
    arrive(sums[1])
    mix_ref[...] = (
        contrib[SLOT[0]].astype(F32)
        + rs_in[SLOT[1]].astype(F32)
        + rs_in[SLOT[-1]].astype(F32)
    ).astype(BF)
    for one in started:
        one.wait_send()


COPIES = 6 + 36 + 14 + 6 + 6 + 7


def on_device(
    q, k, v, strength, rate, factor, extra, s0, residual, seg, routes, gain, router, gate, up, down
):
    vmem = pl.BlockSpec(memory_space=pltpu.VMEM)
    hbm = pl.BlockSpec(memory_space=pl.ANY)
    V = pltpu.VMEM
    return pl.pallas_call(
        kernel,
        out_shape=(
            jax.ShapeDtypeStruct((CHUNKS * C, C), BF),
            jax.ShapeDtypeStruct((1, 1, C, C), F32),
            jax.ShapeDtypeStruct((TOK, D), BF),
        ),
        in_specs=[vmem] * 13 + [hbm] * 3,
        out_specs=(vmem, vmem, vmem),
        scratch_shapes=[
            V((2, SHARDS, DEPTH, FE), BF),
            V((2, SHARDS, DEPTH, FE), BF),
            V((LOCAL, D, FE), BF),
            V((LOCAL, D, FE), BF),
            V((LOCAL, FE, D), BF),
            V((2, DEPTH, FE), BF),
            V((WIDTH, D), BF),
            V((WINDOW, TOK, D), BF),
            V((WINDOW, EXPERTS, TOK), BF),
            V((WINDOW, 8, TOK), F32),
            V((WINDOW, 8, TOK), F32),
            V((LOCAL, 4 * CAP, D), BF),
            V((LOCAL, 4 * CAP, D), BF),
            V((WINDOW, TOK, D), BF),
            V((WINDOW, TOK, D), BF),
            V((WINDOW, TOK, D), BF),
            V((CHUNKS, 2 * C, C), BF),
            V((CHUNKS, C, C), F32),
            V((CHUNKS, C, C), F32),
            V((CHUNKS, C, C), F32),
            V((C, 2 * C), F32),
            V((SIDE, C, 2 * C), F32),
            V((SIDE, C, 2 * C), F32),
            V((C, C), F32),
            pltpu.SemaphoreType.DMA((COPIES,)),
            pltpu.SemaphoreType.DMA((COPIES,)),
            pltpu.SemaphoreType.DMA((3,)),
        ],
        compiler_params=pltpu.CompilerParams(
            collective_id=0, has_side_effects=True, vmem_limit_bytes=58 << 20
        ),
        cost_estimate=pl.CostEstimate(
            flops=7_000_000_000, bytes_accessed=6_000_000, transcendentals=2_000_000
        ),
    )(
        q, k, v,
        strength.reshape(CHUNKS, C), rate, factor.reshape(CHUNKS, C), extra.reshape(CHUNKS, C),
        s0, residual, seg.reshape(1, TOK), routes, gain, router, gate, up, down,
    )


def solution(mesh):
    placed = (
        P("ctx", "exp"), P("ctx", "exp"), P("ctx", "exp"), P("exp", "ctx"), P("exp", None),
        P("exp", "ctx"), P("exp", "ctx"), P("exp", None, None), P(("ctx", "exp"), None),
        P(("ctx", "exp")), P(("ctx", "exp"), None), P(), P(),
        P("exp", "ctx", None), P("exp", "ctx", None), P("exp", "ctx", None),
    )
    return jax.shard_map(
        on_device,
        mesh=mesh,
        in_specs=placed,
        out_specs=(P("ctx", "exp"), P("ctx", "exp", None, None), P(("ctx", "exp"), None)),
        check_vma=False,
    )
```

```python
import functools

import jax
import jax.numpy as jnp
from jax import lax
from jax.experimental import pallas as pl
from jax.experimental.pallas import tpu as pltpu
from jax.sharding import PartitionSpec as P

F32 = jnp.float32
BF = jnp.bfloat16
MESH = pl.DeviceIdType.MESH

C = 128
CHUNKS = 8
TOK = 128
CAP = 40
EXPERTS = 32
MODAL = 3
D = 1152
FE = 512
SIDE = 4
SHARDS = SIDE * SIDE
DEPTH = D // SHARDS
WIDTH = FE // SHARDS
WINDOW = 8
LOCAL = 4
route_scale = 2.446
norm_eps = 1e-06

SLOT = {4: 0, -3: 1, 3: 2, -2: 3, 2: 4, -1: 5, 1: 6, 0: 7}


def dn(a, b, ca, cb):
    return lax.dot_general(
        a.astype(BF), b.astype(BF), (((ca,), (cb,)), ((), ())), preferred_element_type=F32
    )


def split(a):
    high = a.astype(BF)
    return high, (a - high.astype(F32)).astype(BF)


def dot3(a, b):
    ah, al = split(a)
    bh, bl = split(b)
    return dn(ah, bh, 1, 0) + dn(ah, bl, 1, 0) + dn(al, bh, 1, 0)


def unit(v):
    return v * lax.rsqrt(jnp.sum(v * v, axis=-1, keepdims=True) + norm_eps)


def iotas(shape):
    return (
        lax.broadcasted_iota(jnp.int32, shape, 0),
        lax.broadcasted_iota(jnp.int32, shape, 1),
    )


def chunk_terms(n, q_ref, k_ref, v_ref, f_ref, x_ref, b_ref, rate_ref, readers, inner, added, decay):
    row, col = iotas((C, C))
    rows = pl.ds(pl.multiple_of(n * C, C), C)
    ku = unit(k_ref[rows, :].astype(F32))
    qu = unit(q_ref[rows, :].astype(F32))
    v = v_ref[rows, :].astype(F32)
    f = f_ref[pl.ds(n, 1), :]
    x = x_ref[pl.ds(n, 1), :]
    b = b_ref[pl.ds(n, 1), :]
    fc = jnp.sum(jnp.where(col <= row, f, 0.0), axis=1, keepdims=True)
    xc = jnp.sum(jnp.where(col <= row, x, 0.0), axis=1, keepdims=True)
    bc = jnp.sum(jnp.where(col == row, b, 0.0), axis=1, keepdims=True)
    cum = -(rate_ref[0:1, :] * fc + xc)
    last = cum[C - 1 : C, :]
    grown = jnp.exp(cum)
    kg = ku * grown
    ks = ku * jnp.exp(-cum)
    qg = qu * grown
    ke = ku * jnp.exp(last - cum)
    scores = dn(jnp.concatenate([kg, qg], 0), ks, 1, 1)
    a = jnp.where(col < row, scores[:C] * bc, 0.0)
    low = jnp.where(col <= row, scores[C:], 0.0)
    eye = jnp.where(col == row, 1.0, 0.0)
    inverse = eye - a
    square = dn(a, a, 1, 0)
    for level in range(6):
        if level < 5:
            r = dn(jnp.concatenate([inverse, square], 0), square, 1, 0)
            inverse = inverse + r[:C]
            square = r[C:]
        else:
            inverse = inverse + dn(inverse, square, 1, 0)
    solved = dn(inverse, jnp.concatenate([v * bc, kg * bc], 1), 1, 0)
    r1 = dn(low, solved, 1, 0)
    r2 = dn(ke, solved, 0, 0)
    inner[n] = r1[:, :C]
    readers[n] = jnp.concatenate([(qg - r1[:, C:]).astype(BF), r2[:, C:].astype(BF)], 0)
    added[n] = r2[:, :C]
    column = jnp.sum(jnp.where(col == row, jnp.exp(last), 0.0), axis=1, keepdims=True)
    decay[n] = jnp.broadcast_to(column, (C, C))


def kernel(
    q_ref, k_ref, v_ref, b_ref, rate_ref, f_ref, x_ref, s0_ref, res_ref, seg_ref, routes_ref,
    gain_ref, router_ref, gate_ref, up_ref, down_ref,
    att_ref, state_ref, mix_ref,
    gs, us, wg, wu, wd, tok, table, slot_ids, slot_w, xin, eo, contrib, rs_out,
    rs_in, readers, inner, added, decay, gmap, rowmaps, colmaps, state, send_sem, recv_sem, loc_sem,
):
    ctx = lax.axis_index("ctx")
    own = lax.axis_index("exp")
    px, py = ctx // SIDE, ctx % SIDE
    pz, core = own // 2, own % 2
    planes = EXPERTS // 2
    sense = 1 - 2 * core

    def along_z(steps):
        return (ctx, lax.rem(pz + sense * steps + planes, planes) * 2 + core)

    def along_x(steps):
        return (lax.rem(px + sense * steps + SIDE, SIDE) * SIDE + py, own)

    def along_y(steps):
        return (px * SIDE + lax.rem(py + sense * steps + SIDE, SIDE), own)

    def along_column(steps):
        return (lax.rem(px + steps, SIDE) * SIDE + py, own)

    def along_row(steps):
        return (px * SIDE + lax.rem(py + steps, SIDE), own)

    sibling = (ctx, pz * 2 + 1 - core)
    ids = {}

    def remote(name, src, dst, device):
        k = ids.setdefault(name, len(ids))
        return pltpu.make_async_remote_copy(
            src_ref=src, dst_ref=dst, send_sem=send_sem.at[k], recv_sem=recv_sem.at[k],
            device_id=device, device_id_type=MESH,
        )

    started = []

    def go(copies):
        for one in copies:
            one.start()
        started.extend(copies)
        return copies

    def arrive(copies):
        for one in copies:
            one.wait_recv()

    barrier = pltpu.get_barrier_semaphore()
    partners = [along_z(t) for t in (1, -1, 8)] + [sibling]
    partners += [along_column(t) for t in (1, 2, 3)] + [along_row(t) for t in (1, 2, 3)]
    for device in partners:
        pl.semaphore_signal(barrier, inc=1, device_id=device, device_id_type=MESH)
    pl.semaphore_wait(barrier, len(partners))

    HALF = FE // 2
    pieces = {}
    for r in range(2):
        pieces["g", r] = (
            lambda i, r=r: gs.at[r, i],
            lambda i, r=r: gs.at[r, pl.ds(i * SIDE, SIDE)],
            gate_ref.at[0], True,
        )
        for half in range(2):
            cols = pl.ds(half * HALF, HALF)
            pieces[f"u{half}", r] = (
                lambda i, r=r, cols=cols: us.at[r, i, :, cols],
                lambda i, r=r, cols=cols: us.at[r, pl.ds(i * SIDE, SIDE), :, cols],
                up_ref.at[0, :, cols], half == 0,
            )
        pieces["d", r] = (
            lambda i, r=r: wd.at[2 * r, pl.ds(pl.multiple_of(i * WIDTH, WIDTH), WIDTH)],
            lambda i, r=r: wd.at[
                2 * r, pl.ds(pl.multiple_of(i * SIDE * WIDTH, SIDE * WIDTH), SIDE * WIDTH)
            ],
            down_ref.at[0], False,
        )
    moves = {}

    def place(key):
        x_first = pieces[key][3]
        return (px, py, along_x, along_y) if x_first else (py, px, along_y, along_x)

    def near(key):
        one, block, given, x_first = pieces[key]
        a, b, axis, other = place(key)
        here = one(b * SIDE + a)
        src = given if key[1] == 0 else here
        moves[key] = [
            remote(f"{key}p", src, here, axis(1)), remote(f"{key}m", src, here, axis(-1))
        ]
        go(moves[key])

    def near_on(key):
        one, block, given, x_first = pieces[key]
        a, b, axis, other = place(key)
        arrive(moves[key][:1])
        from_behind = one(b * SIDE + lax.rem(a - sense + SIDE, SIDE))
        moves[key].append(remote(f"{key}f", from_behind, from_behind, axis(1)))
        go(moves[key][2:])

    def far(key):
        one, block, given, x_first = pieces[key]
        a, b, axis, other = place(key)
        arrive(moves[key][1:])
        line = block(b)
        moves[key] = [
            remote(f"{key}P", line, line, other(1)), remote(f"{key}M", line, line, other(-1))
        ]
        go(moves[key])

    def far_on(key):
        one, block, given, x_first = pieces[key]
        a, b, axis, other = place(key)
        arrive(moves[key][:1])
        line = block(lax.rem(b - sense + SIDE, SIDE))
        moves[key].append(remote(f"{key}F", line, line, other(1)))
        go(moves[key][2:])

    def complete(key):
        arrive(moves[key][1:])

    KINDS = ("g", "u0", "u1", "d")
    across = {}
    locals_ = []

    def cross(kind):
        one, block, given, x_first = pieces[kind, 1]
        a, b, axis, other = place((kind, 1))
        across[kind] = go([remote(f"{kind}z", given, one(b * SIDE + a), along_z(8))])

    for kind in KINDS:
        cross(kind)
    for n, kind in enumerate(KINDS):
        one, block, given, x_first = pieces[kind, 0]
        a, b, axis, other = place((kind, 0))
        near((kind, 0))
        locals_.append(pltpu.make_async_copy(given, one(b * SIDE + a), loc_sem.at[n]))
        locals_[-1].start()

    def each(step, r, kinds=KINDS):
        for kind in kinds:
            step((kind, r))

    def crossed_one(key):
        arrive(across[key[0]])
        near(key)

    row, col = iotas((C, C))
    stream = res_ref[...].astype(F32)
    scale = lax.rsqrt(jnp.mean(stream * stream, axis=1, keepdims=True) + norm_eps)
    seg = seg_ref[...].astype(F32)
    modality = seg - MODAL * jnp.floor((seg + 0.5) * (1.0 / MODAL))
    modality = jnp.sum(jnp.where(col == row, modality, 0.0), axis=1, keepdims=True)
    gains = jnp.where(
        modality == 0.0,
        gain_ref[0:1, :],
        jnp.where(modality == 1.0, gain_ref[1:2, :], gain_ref[2:3, :]),
    )
    normed = (stream * scale * gains).astype(BF)
    tok[SLOT[0]] = normed
    logits = dn(normed, router_ref[...], 1, 0)
    lane = lax.broadcasted_iota(jnp.int32, (TOK, EXPERTS), 1)
    hits = jnp.zeros((TOK, EXPERTS), F32)
    routes = routes_ref[...]
    for turn in range(8):
        hits = hits + jnp.where(routes[:, turn : turn + 1] == lane, 1.0, 0.0)
    scores = jnp.where(hits > 0.0, 1.0 / (1.0 + jnp.exp(-logits)), 0.0)
    weights = route_scale * scores / jnp.sum(scores, axis=1, keepdims=True)
    wide = jnp.concatenate([weights, jnp.zeros((TOK, C - EXPERTS), F32)], 1)
    table[SLOT[0]] = jnp.transpose(wide)[:EXPERTS].astype(BF)

    def token_step(way, k, half):
        src, dst = SLOT[way * (k - 1)], SLOT[way * k]
        part = pl.ds(half * (TOK // 2), TOK // 2)
        copies = []
        if half == 0:
            copies.append(remote(f"w{way}{k}", table.at[src], table.at[dst], along_z(way)))
        copies.append(
            remote(f"t{way}{k}{half}", tok.at[src, part], tok.at[dst, part], along_z(way))
        )
        return go(copies)

    hops = {}

    def first_hop():
        for half in range(2):
            for way in (1, -1):
                hops[way, 1, half] = token_step(way, 1, half)

    def pass_on(k):
        for half in range(2):
            for way, last in ((1, 4), (-1, 3)):
                if k <= last:
                    arrive(hops[way, k, half])
                if k < last:
                    hops[way, k + 1, half] = token_step(way, k + 1, half)

    def chunks(lo, hi):
        def body(n, carry):
            chunk_terms(
                n, q_ref, k_ref, v_ref, f_ref, x_ref, b_ref, rate_ref, readers, inner, added, decay
            )
            return carry

        lax.fori_loop(lo, hi, body, 0)

    def merge(src, r, dst, kinds):
        def body(h, carry):
            at = pl.ds(pl.multiple_of(h * 2 * DEPTH, 2 * DEPTH), 2 * DEPTH)
            for lo, hi, x_first in kinds:
                parts = []
                for late in range(2):
                    i = 2 * h + late
                    where = (i % SIDE) * SIDE + i // SIDE if x_first else i
                    parts.append(src[r, where, :, lo:hi].astype(F32))
                dst[2 * r, at, lo:hi] = jnp.concatenate(parts, 0).astype(BF)
            return carry

        lax.fori_loop(0, SHARDS // 2, body, 0)

    GATE_KINDS = [(0, FE, True)]
    UP_KINDS = [(0, HALF, True), (HALF, FE, False)]

    def share(kind, held, r):
        return go([remote(f"s{kind}{r}", held.at[2 * r], held.at[2 * r + 1], sibling)])

    def outputs(n, carry):
        s = state[...]
        r = dn(readers[n], s, 1, 0)
        att_ref[pl.ds(pl.multiple_of(n * C, C), C), :] = (inner[n] + r[:C]).astype(BF)
        state[...] = decay[n] * s - r[C:] + added[n]
        return carry

    upper = jnp.where(row <= col, 1.0, 0.0)
    pick_row, pick_col = iotas((8, EXPERTS))
    mine = []
    for r in range(2):
        plane = lax.rem(pz + 8 * r, planes)
        mine += [2 * plane + core, 2 * plane + 1 - core]
    select = jnp.zeros((8, EXPERTS), F32)
    for e in range(LOCAL):
        select = select + jnp.where((pick_row == e) & (pick_col == mine[e]), 1.0, 0.0)

    PAIR = 2 * CAP
    place_rows = lax.broadcasted_iota(jnp.int32, (PAIR, 2 * TOK), 0).astype(F32)

    def spread(pair, weighted):
        a, b = 2 * pair, 2 * pair + 1
        parts = []
        for e in range(LOCAL):
            ids_row = jnp.concatenate([slot_ids[a, e : e + 1, :], slot_ids[b, e : e + 1, :]], 1)
            if weighted:
                value = jnp.concatenate([slot_w[a, e : e + 1, :], slot_w[b, e : e + 1, :]], 1)
            else:
                value = 1.0
            parts.append(jnp.where(place_rows == ids_row, value, 0.0))
        return jnp.concatenate(parts, 0).astype(BF)

    def gather(group):
        for half in range(2):
            pair = 2 * group + half
            for slot in (2 * pair, 2 * pair + 1):
                w = dn(select, table[slot], 1, 0)
                hit = w != 0.0
                count = dn(jnp.where(hit, 1.0, 0.0), upper, 1, 0)
                slot_ids[slot] = jnp.where(hit, count + (CAP * (slot % 2) - 1.0), -1.0)
                slot_w[slot] = w
            both = tok[2 * pair : 2 * pair + 2].reshape(2 * TOK, D)
            rows = dn(spread(pair, False), both, 1, 0).astype(BF)
            for e in range(LOCAL):
                xin[e, pair * PAIR : (pair + 1) * PAIR, :] = rows[e * PAIR : (e + 1) * PAIR]

    def experts(lo, hi, first, last):
        def body(e, carry):
            x = xin[e, first:last, :]
            g = dn(x, wg[e], 1, 0)
            u = dn(x, wu[e], 1, 0)
            hidden = (g / (1.0 + jnp.exp(-g)) * u).astype(BF)
            eo[e, first:last, :] = dn(hidden, wd[e], 1, 0).astype(BF)
            return carry

        if hi - lo == 1:
            body(lo, 0)
        else:
            lax.fori_loop(lo, hi, body, 0)

    def combine(group):
        for half in range(2):
            pair = 2 * group + half
            made = jnp.concatenate(
                [eo[e, pair * PAIR : (pair + 1) * PAIR, :] for e in range(LOCAL)], 0
            )
            both = dn(spread(pair, True), made, 0, 0)
            contrib[2 * pair] = both[:TOK].astype(BF)
            contrib[2 * pair + 1] = both[TOK:].astype(BF)

    each(near_on, 0)
    chunks(0, 2)
    for one in locals_:
        one.wait()
    each(far, 0)
    chunks(2, 8)
    gmap[...] = jnp.concatenate([jnp.zeros((C, C), F32), jnp.where(col == row, 1.0, 0.0)], 1)

    def grow(n, carry):
        d = decay[n]
        m = gmap[...]
        r = dn(readers[n, C:], m, 1, 0)
        gmap[...] = jnp.concatenate(
            [d * m[:, :C] - r[:, :C] + added[n], d * m[:, C:] - r[:, C:]], 1
        )
        return carry

    lax.fori_loop(0, CHUNKS, grow, 0)
    rowmaps[py] = gmap[...]
    row_copies = go([
        remote(f"r{t}", gmap, rowmaps.at[py], along_row(t)) for t in (1, 3, 2)
    ])
    each(far_on, 0)
    each(crossed_one, 1)
    first_hop()
    arrive(row_copies)
    whole = rowmaps[0]
    for t in range(1, SIDE):
        m = rowmaps[t]
        whole = dot3(m[:, C:], whole)
        whole = jnp.concatenate([whole[:, :C] + m[:, :C], whole[:, C:]], 1)
    colmaps[px] = whole
    col_copies = go([
        remote(f"c{t}", colmaps.at[px], colmaps.at[px], along_column(t)) for t in (1, 3, 2)
    ])
    each(near_on, 1)
    each(far, 1)
    pass_on(1)
    each(complete, 0)
    merge(gs, 0, wg, GATE_KINDS)
    merge(us, 0, wu, UP_KINDS)
    share_own = share("g", wg, 0) + share("u", wu, 0) + share("d", wd, 0)
    arrive(col_copies)
    entering = s0_ref[0]
    for t in range(SIDE - 1):
        m = colmaps[t]
        entering = jnp.where(px > t, dot3(m[:, C:], entering) + m[:, :C], entering)
    for t in range(SIDE - 1):
        m = rowmaps[t]
        entering = jnp.where(py > t, dot3(m[:, C:], entering) + m[:, :C], entering)
    state[...] = entering
    pass_on(2)
    each(far_on, 1)
    gather(1)
    arrive(share_own)
    ROWS = WINDOW * CAP
    experts(0, 2, ROWS // 2, ROWS)
    pass_on(3)
    lax.fori_loop(0, CHUNKS, outputs, 0)
    state_ref[0, 0] = state[...]
    complete(("g", 1))
    merge(gs, 1, wg, GATE_KINDS)
    share_gate = share("g", wg, 1)
    complete(("u0", 1))
    complete(("u1", 1))
    merge(us, 1, wu, UP_KINDS)
    share_up = share("u", wu, 1)
    complete(("d", 1))
    share_down = share("d", wd, 1)
    pass_on(4)
    gather(0)
    experts(0, 2, 0, ROWS // 2)
    experts(2, 3, 0, ROWS)
    arrive(share_gate + share_up + share_down)
    experts(3, 4, 0, ROWS)
    combine(0)

    sums = {}

    def send_sum(distance):
        way = -1 if distance > 0 else 1
        at = SLOT[distance]
        for half in range(2):
            part = pl.ds(half * (TOK // 2), TOK // 2)
            if distance in (4, -3):
                src = contrib.at[at, part]
            else:
                arrive(sums[distance - way, half])
                inbox = SLOT[distance - way]
                rs_out[at, part, :] = (
                    contrib[at, part, :].astype(F32) + rs_in[inbox, part, :].astype(F32)
                ).astype(BF)
                src = rs_out.at[at, part]
            sums[distance, half] = go([
                remote(f"s{distance}{half}", src, rs_in.at[at, part], along_z(way))
            ])

    send_sum(4)
    send_sum(-3)
    combine(1)

    send_sum(3)
    send_sum(-2)
    send_sum(2)
    send_sum(-1)
    send_sum(1)
    for half in range(2):
        part = pl.ds(half * (TOK // 2), TOK // 2)
        arrive(sums[-1, half] + sums[1, half])
        mix_ref[part, :] = (
            contrib[SLOT[0], part, :].astype(F32)
            + rs_in[SLOT[1], part, :].astype(F32)
            + rs_in[SLOT[-1], part, :].astype(F32)
        ).astype(BF)
    for one in started:
        one.wait_send()


COPIES = 4 + 48 + 21 + 6 + 6 + 14


def on_device(
    q, k, v, strength, rate, factor, extra, s0, residual, seg, routes, gain, router, gate, up, down
):
    vmem = pl.BlockSpec(memory_space=pltpu.VMEM)
    hbm = pl.BlockSpec(memory_space=pl.ANY)
    V = pltpu.VMEM
    return pl.pallas_call(
        kernel,
        out_shape=(
            jax.ShapeDtypeStruct((CHUNKS * C, C), BF),
            jax.ShapeDtypeStruct((1, 1, C, C), F32),
            jax.ShapeDtypeStruct((TOK, D), BF),
        ),
        in_specs=[vmem] * 13 + [hbm] * 3,
        out_specs=(vmem, vmem, vmem),
        scratch_shapes=[
            V((2, SHARDS, DEPTH, FE), BF),
            V((2, SHARDS, DEPTH, FE), BF),
            V((LOCAL, D, FE), BF),
            V((LOCAL, D, FE), BF),
            V((LOCAL, FE, D), BF),
            V((WINDOW, TOK, D), BF),
            V((WINDOW, EXPERTS, TOK), BF),
            V((WINDOW, 8, TOK), F32),
            V((WINDOW, 8, TOK), F32),
            V((LOCAL, WINDOW * CAP, D), BF),
            V((LOCAL, WINDOW * CAP, D), BF),
            V((WINDOW, TOK, D), BF),
            V((WINDOW, TOK, D), BF),
            V((WINDOW, TOK, D), BF),
            V((CHUNKS, 2 * C, C), BF),
            V((CHUNKS, C, C), F32),
            V((CHUNKS, C, C), F32),
            V((CHUNKS, C, C), F32),
            V((C, 2 * C), F32),
            V((SIDE, C, 2 * C), F32),
            V((SIDE, C, 2 * C), F32),
            V((C, C), F32),
            pltpu.SemaphoreType.DMA((COPIES,)),
            pltpu.SemaphoreType.DMA((COPIES,)),
            pltpu.SemaphoreType.DMA((4,)),
        ],
        compiler_params=pltpu.CompilerParams(
            collective_id=0, has_side_effects=True, vmem_limit_bytes=58 << 20
        ),
        cost_estimate=pl.CostEstimate(
            flops=7_000_000_000, bytes_accessed=6_000_000, transcendentals=2_000_000
        ),
    )(
        q, k, v,
        strength.reshape(CHUNKS, C), rate, factor.reshape(CHUNKS, C), extra.reshape(CHUNKS, C),
        s0, residual, seg.reshape(1, TOK), routes, gain, router, gate, up, down,
    )


def solution(mesh):
    placed = (
        P("ctx", "exp"), P("ctx", "exp"), P("ctx", "exp"), P("exp", "ctx"), P("exp", None),
        P("exp", "ctx"), P("exp", "ctx"), P("exp", None, None), P(("ctx", "exp"), None),
        P(("ctx", "exp")), P(("ctx", "exp"), None), P(), P(),
        P("exp", "ctx", None), P("exp", "ctx", None), P("exp", "ctx", None),
    )
    return jax.shard_map(
        on_device,
        mesh=mesh,
        in_specs=placed,
        out_specs=(P("ctx", "exp"), P("ctx", "exp", None, None), P(("ctx", "exp"), None)),
        check_vma=False,
    )
```

```python
import functools

import jax
import jax.numpy as jnp
from jax import lax
from jax.experimental import pallas as pl
from jax.experimental.pallas import tpu as pltpu
from jax.sharding import PartitionSpec as P

F32 = jnp.float32
BF = jnp.bfloat16
MESH = pl.DeviceIdType.MESH

C = 128
CHUNKS = 8
TOK = 128
CAP = 40
EXPERTS = 32
MODAL = 3
D = 1152
FE = 512
SIDE = 4
SHARDS = SIDE * SIDE
DEPTH = D // SHARDS
WIDTH = FE // SHARDS
WINDOW = 8
LOCAL = 4
route_scale = 2.446
norm_eps = 1e-06

SLOT = {4: 0, -3: 1, 3: 2, -2: 3, 2: 4, -1: 5, 1: 6, 0: 7}


def dn(a, b, ca, cb):
    return lax.dot_general(
        a.astype(BF), b.astype(BF), (((ca,), (cb,)), ((), ())), preferred_element_type=F32
    )


def split(a):
    high = a.astype(BF)
    return high, (a - high.astype(F32)).astype(BF)


def dot3(a, b):
    ah, al = split(a)
    bh, bl = split(b)
    return dn(ah, bh, 1, 0) + dn(ah, bl, 1, 0) + dn(al, bh, 1, 0)


def unit(v):
    return v * lax.rsqrt(jnp.sum(v * v, axis=-1, keepdims=True) + norm_eps)


def iotas(shape):
    return (
        lax.broadcasted_iota(jnp.int32, shape, 0),
        lax.broadcasted_iota(jnp.int32, shape, 1),
    )


def chunk_terms(n, q_ref, k_ref, v_ref, f_ref, x_ref, b_ref, rate_ref, readers, inner, added, decay):
    row, col = iotas((C, C))
    rows = pl.ds(pl.multiple_of(n * C, C), C)
    ku = unit(k_ref[rows, :].astype(F32))
    qu = unit(q_ref[rows, :].astype(F32))
    v = v_ref[rows, :].astype(F32)
    f = f_ref[pl.ds(n, 1), :]
    x = x_ref[pl.ds(n, 1), :]
    b = b_ref[pl.ds(n, 1), :]
    fc = jnp.sum(jnp.where(col <= row, f, 0.0), axis=1, keepdims=True)
    xc = jnp.sum(jnp.where(col <= row, x, 0.0), axis=1, keepdims=True)
    bc = jnp.sum(jnp.where(col == row, b, 0.0), axis=1, keepdims=True)
    cum = -(rate_ref[0:1, :] * fc + xc)
    last = cum[C - 1 : C, :]
    grown = jnp.exp(cum)
    kg = ku * grown
    ks = ku * jnp.exp(-cum)
    qg = qu * grown
    ke = ku * jnp.exp(last - cum)
    scores = dn(jnp.concatenate([kg, qg], 0), ks, 1, 1)
    a = jnp.where(col < row, scores[:C] * bc, 0.0)
    low = jnp.where(col <= row, scores[C:], 0.0)
    eye = jnp.where(col == row, 1.0, 0.0)
    inverse = eye - a
    square = dn(a, a, 1, 0)
    for level in range(6):
        if level < 5:
            r = dn(jnp.concatenate([inverse, square], 0), square, 1, 0)
            inverse = inverse + r[:C]
            square = r[C:]
        else:
            inverse = inverse + dn(inverse, square, 1, 0)
    solved = dn(inverse, jnp.concatenate([v * bc, kg * bc], 1), 1, 0)
    r1 = dn(low, solved, 1, 0)
    r2 = dn(ke, solved, 0, 0)
    inner[n] = r1[:, :C]
    readers[n] = jnp.concatenate([(qg - r1[:, C:]).astype(BF), r2[:, C:].astype(BF)], 0)
    added[n] = r2[:, :C]
    column = jnp.sum(jnp.where(col == row, jnp.exp(last), 0.0), axis=1, keepdims=True)
    decay[n] = jnp.broadcast_to(column, (C, C))


def kernel(
    q_ref, k_ref, v_ref, b_ref, rate_ref, f_ref, x_ref, s0_ref, res_ref, seg_ref, routes_ref,
    gain_ref, router_ref, gate_ref, up_ref, down_ref,
    att_ref, state_ref, mix_ref,
    gs, us, wg, wu, wd, tok, table, slot_ids, slot_w, xin, eo, contrib, rs_out,
    rs_in, readers, inner, added, decay, gmap, rowmaps, colmaps, state, send_sem, recv_sem, loc_sem,
):
    ctx = lax.axis_index("ctx")
    own = lax.axis_index("exp")
    px, py = ctx // SIDE, ctx % SIDE
    pz, core = own // 2, own % 2
    planes = EXPERTS // 2
    sense = 1 - 2 * core

    def along_z(steps):
        return (ctx, lax.rem(pz + sense * steps + planes, planes) * 2 + core)

    def along_x(steps):
        return (lax.rem(px + sense * steps + SIDE, SIDE) * SIDE + py, own)

    def along_y(steps):
        return (px * SIDE + lax.rem(py + sense * steps + SIDE, SIDE), own)

    def along_column(steps):
        return (lax.rem(px + steps, SIDE) * SIDE + py, own)

    def along_row(steps):
        return (px * SIDE + lax.rem(py + steps, SIDE), own)

    sibling = (ctx, pz * 2 + 1 - core)
    ids = {}

    def remote(name, src, dst, device):
        k = ids.setdefault(name, len(ids))
        return pltpu.make_async_remote_copy(
            src_ref=src, dst_ref=dst, send_sem=send_sem.at[k], recv_sem=recv_sem.at[k],
            device_id=device, device_id_type=MESH,
        )

    started = []

    def go(copies):
        for one in copies:
            one.start()
        started.extend(copies)
        return copies

    def arrive(copies):
        for one in copies:
            one.wait_recv()

    barrier = pltpu.get_barrier_semaphore()
    partners = [along_z(t) for t in (1, -1, 8)] + [sibling]
    partners += [along_column(t) for t in (1, 2, 3)] + [along_row(t) for t in (1, 2, 3)]
    for device in partners:
        pl.semaphore_signal(barrier, inc=1, device_id=device, device_id_type=MESH)
    pl.semaphore_wait(barrier, len(partners))

    HALF = FE // 2
    pieces = {}
    for r in range(2):
        pieces["g", r] = (
            lambda i, r=r: gs.at[r, i],
            lambda i, r=r: gs.at[r, pl.ds(i * SIDE, SIDE)],
            gate_ref.at[0], True,
        )
        for half in range(2):
            cols = pl.ds(half * HALF, HALF)
            pieces[f"u{half}", r] = (
                lambda i, r=r, cols=cols: us.at[r, i, :, cols],
                lambda i, r=r, cols=cols: us.at[r, pl.ds(i * SIDE, SIDE), :, cols],
                up_ref.at[0, :, cols], half == 0,
            )
        pieces["d", r] = (
            lambda i, r=r: wd.at[2 * r, pl.ds(pl.multiple_of(i * WIDTH, WIDTH), WIDTH)],
            lambda i, r=r: wd.at[
                2 * r, pl.ds(pl.multiple_of(i * SIDE * WIDTH, SIDE * WIDTH), SIDE * WIDTH)
            ],
            down_ref.at[0], False,
        )
    moves = {}

    def place(key):
        x_first = pieces[key][3]
        return (px, py, along_x, along_y) if x_first else (py, px, along_y, along_x)

    def near(key):
        one, block, given, x_first = pieces[key]
        a, b, axis, other = place(key)
        here = one(b * SIDE + a)
        src = given if key[1] == 0 else here
        moves[key] = [
            remote(f"{key}p", src, here, axis(1)), remote(f"{key}m", src, here, axis(-1))
        ]
        go(moves[key])

    def near_on(key):
        one, block, given, x_first = pieces[key]
        a, b, axis, other = place(key)
        arrive(moves[key][:1])
        from_behind = one(b * SIDE + lax.rem(a - sense + SIDE, SIDE))
        moves[key].append(remote(f"{key}f", from_behind, from_behind, axis(1)))
        go(moves[key][2:])

    def far(key):
        one, block, given, x_first = pieces[key]
        a, b, axis, other = place(key)
        arrive(moves[key][1:])
        line = block(b)
        moves[key] = [
            remote(f"{key}P", line, line, other(1)), remote(f"{key}M", line, line, other(-1))
        ]
        go(moves[key])

    def far_on(key):
        one, block, given, x_first = pieces[key]
        a, b, axis, other = place(key)
        arrive(moves[key][:1])
        line = block(lax.rem(b - sense + SIDE, SIDE))
        moves[key].append(remote(f"{key}F", line, line, other(1)))
        go(moves[key][2:])

    def complete(key):
        arrive(moves[key][1:])

    KINDS = ("g", "u0", "u1", "d")
    across = {}
    locals_ = []

    def cross(kind):
        one, block, given, x_first = pieces[kind, 1]
        a, b, axis, other = place((kind, 1))
        across[kind] = go([remote(f"{kind}z", given, one(b * SIDE + a), along_z(8))])

    for kind in KINDS:
        cross(kind)
    for n, kind in enumerate(KINDS):
        one, block, given, x_first = pieces[kind, 0]
        a, b, axis, other = place((kind, 0))
        near((kind, 0))
        locals_.append(pltpu.make_async_copy(given, one(b * SIDE + a), loc_sem.at[n]))
        locals_[-1].start()

    def each(step, r, kinds=KINDS):
        for kind in kinds:
            step((kind, r))

    def crossed_one(key):
        arrive(across[key[0]])
        near(key)

    row, col = iotas((C, C))
    stream = res_ref[...].astype(F32)
    scale = lax.rsqrt(jnp.mean(stream * stream, axis=1, keepdims=True) + norm_eps)
    seg = seg_ref[...].astype(F32)
    modality = seg - MODAL * jnp.floor((seg + 0.5) * (1.0 / MODAL))
    modality = jnp.sum(jnp.where(col == row, modality, 0.0), axis=1, keepdims=True)
    gains = jnp.where(
        modality == 0.0,
        gain_ref[0:1, :],
        jnp.where(modality == 1.0, gain_ref[1:2, :], gain_ref[2:3, :]),
    )
    normed = (stream * scale * gains).astype(BF)
    tok[SLOT[0]] = normed
    logits = dn(router_ref[...], normed, 1, 1)
    expert = lax.broadcasted_iota(jnp.int32, (EXPERTS, TOK), 0)
    hits = jnp.zeros((EXPERTS, TOK), F32)
    for turn in range(8):
        hits = hits + jnp.where(routes_ref[turn : turn + 1, :] == expert, 1.0, 0.0)
    scores = jnp.where(hits > 0.0, 1.0 / (1.0 + jnp.exp(-logits)), 0.0)
    weights = route_scale * scores / jnp.sum(scores, axis=0, keepdims=True)
    table[SLOT[0]] = weights.astype(BF)

    def token_step(way, k, half):
        src, dst = SLOT[way * (k - 1)], SLOT[way * k]
        part = pl.ds(half * (TOK // 2), TOK // 2)
        copies = []
        if half == 0:
            copies.append(remote(f"w{way}{k}", table.at[src], table.at[dst], along_z(way)))
        copies.append(
            remote(f"t{way}{k}{half}", tok.at[src, part], tok.at[dst, part], along_z(way))
        )
        return go(copies)

    hops = {}

    def first_hop():
        for half in range(2):
            for way in (1, -1):
                hops[way, 1, half] = token_step(way, 1, half)

    def pass_on(k):
        for half in range(2):
            for way, last in ((1, 4), (-1, 3)):
                if k <= last:
                    arrive(hops[way, k, half])
                if k < last:
                    hops[way, k + 1, half] = token_step(way, k + 1, half)

    def chunks(lo, hi):
        def body(n, carry):
            chunk_terms(
                n, q_ref, k_ref, v_ref, f_ref, x_ref, b_ref, rate_ref, readers, inner, added, decay
            )
            return carry

        lax.fori_loop(lo, hi, body, 0)

    def merge(src, r, dst, kinds):
        def body(h, carry):
            at = pl.ds(pl.multiple_of(h * 2 * DEPTH, 2 * DEPTH), 2 * DEPTH)
            for lo, hi, x_first in kinds:
                parts = []
                for late in range(2):
                    i = 2 * h + late
                    where = (i % SIDE) * SIDE + i // SIDE if x_first else i
                    parts.append(src[r, where, :, lo:hi].astype(F32))
                dst[2 * r, at, lo:hi] = jnp.concatenate(parts, 0).astype(BF)
            return carry

        lax.fori_loop(0, SHARDS // 2, body, 0)

    GATE_KINDS = [(0, FE, True)]
    UP_KINDS = [(0, HALF, True), (HALF, FE, False)]

    def share(kind, held, r):
        return go([remote(f"s{kind}{r}", held.at[2 * r], held.at[2 * r + 1], sibling)])

    def outputs(n, carry):
        s = state[...]
        r = dn(readers[n], s, 1, 0)
        att_ref[pl.ds(pl.multiple_of(n * C, C), C), :] = inner[n] + r[:C]
        state[...] = decay[n] * s - r[C:] + added[n]
        return carry

    upper = jnp.where(row <= col, 1.0, 0.0)
    pick_row, pick_col = iotas((8, EXPERTS))
    mine = []
    for r in range(2):
        plane = lax.rem(pz + 8 * r, planes)
        mine += [2 * plane + core, 2 * plane + 1 - core]
    select = jnp.zeros((8, EXPERTS), F32)
    for e in range(LOCAL):
        select = select + jnp.where((pick_row == e) & (pick_col == mine[e]), 1.0, 0.0)

    PAIR = 2 * CAP
    place_rows = lax.broadcasted_iota(jnp.int32, (PAIR, 2 * TOK), 0).astype(F32)

    def spread(pair, weighted):
        a, b = 2 * pair, 2 * pair + 1
        parts = []
        for e in range(LOCAL):
            ids_row = jnp.concatenate([slot_ids[a, e : e + 1, :], slot_ids[b, e : e + 1, :]], 1)
            if weighted:
                value = jnp.concatenate([slot_w[a, e : e + 1, :], slot_w[b, e : e + 1, :]], 1)
            else:
                value = 1.0
            parts.append(jnp.where(place_rows == ids_row, value, 0.0))
        return jnp.concatenate(parts, 0).astype(BF)

    def gather(group):
        for half in range(2):
            pair = 2 * group + half
            for slot in (2 * pair, 2 * pair + 1):
                w = dn(select, table[slot], 1, 0)
                hit = w != 0.0
                count = dn(jnp.where(hit, 1.0, 0.0), upper, 1, 0)
                slot_ids[slot] = jnp.where(hit, count + (CAP * (slot % 2) - 1.0), -1.0)
                slot_w[slot] = w
            both = tok[2 * pair : 2 * pair + 2].reshape(2 * TOK, D)
            rows = dn(spread(pair, False), both, 1, 0).astype(BF)
            for e in range(LOCAL):
                xin[e, pair * PAIR : (pair + 1) * PAIR, :] = rows[e * PAIR : (e + 1) * PAIR]

    def experts(lo, hi, first, last):
        def body(e, carry):
            x = xin[e, first:last, :]
            g = dn(x, wg[e], 1, 0)
            u = dn(x, wu[e], 1, 0)
            hidden = (g / (1.0 + jnp.exp(-g)) * u).astype(BF)
            eo[e, first:last, :] = dn(hidden, wd[e], 1, 0).astype(BF)
            return carry

        if hi - lo == 1:
            body(lo, 0)
        else:
            lax.fori_loop(lo, hi, body, 0)

    def combine(group):
        for half in range(2):
            pair = 2 * group + half
            made = jnp.concatenate(
                [eo[e, pair * PAIR : (pair + 1) * PAIR, :] for e in range(LOCAL)], 0
            )
            both = dn(spread(pair, True), made, 0, 0)
            contrib[2 * pair] = both[:TOK].astype(BF)
            contrib[2 * pair + 1] = both[TOK:].astype(BF)

    each(near_on, 0)
    chunks(0, 2)
    for one in locals_:
        one.wait()
    each(far, 0)
    chunks(2, 8)
    gmap[...] = jnp.concatenate([jnp.zeros((C, C), F32), jnp.where(col == row, 1.0, 0.0)], 1)

    def grow(n, carry):
        d = decay[n]
        m = gmap[...]
        r = dn(readers[n, C:], m, 1, 0)
        gmap[...] = jnp.concatenate(
            [d * m[:, :C] - r[:, :C] + added[n], d * m[:, C:] - r[:, C:]], 1
        )
        return carry

    lax.fori_loop(0, CHUNKS, grow, 0)
    rowmaps[py] = gmap[...]
    row_copies = go([
        remote(f"r{t}", gmap, rowmaps.at[py], along_row(t)) for t in (1, 3, 2)
    ])
    each(far_on, 0)
    each(crossed_one, 1)
    first_hop()
    arrive(row_copies)
    whole = rowmaps[0]
    for t in range(1, SIDE):
        m = rowmaps[t]
        whole = dot3(m[:, C:], whole)
        whole = jnp.concatenate([whole[:, :C] + m[:, :C], whole[:, C:]], 1)
    colmaps[px] = whole
    col_copies = go([
        remote(f"c{t}", colmaps.at[px], colmaps.at[px], along_column(t)) for t in (1, 3, 2)
    ])
    each(near_on, 1)
    each(far, 1)
    pass_on(1)
    each(complete, 0)
    merge(gs, 0, wg, GATE_KINDS)
    merge(us, 0, wu, UP_KINDS)
    share_own = share("g", wg, 0) + share("u", wu, 0) + share("d", wd, 0)
    arrive(col_copies)
    entering = s0_ref[0]
    for t in range(SIDE - 1):
        m = colmaps[t]
        entering = jnp.where(px > t, dot3(m[:, C:], entering) + m[:, :C], entering)
    for t in range(SIDE - 1):
        m = rowmaps[t]
        entering = jnp.where(py > t, dot3(m[:, C:], entering) + m[:, :C], entering)
    state[...] = entering
    pass_on(2)
    each(far_on, 1)
    gather(1)
    arrive(share_own)
    ROWS = WINDOW * CAP
    experts(0, 2, ROWS // 2, ROWS)
    pass_on(3)
    lax.fori_loop(0, CHUNKS, outputs, 0)
    state_ref[0, 0] = state[...]
    complete(("g", 1))
    merge(gs, 1, wg, GATE_KINDS)
    share_gate = share("g", wg, 1)
    complete(("u0", 1))
    complete(("u1", 1))
    merge(us, 1, wu, UP_KINDS)
    share_up = share("u", wu, 1)
    complete(("d", 1))
    share_down = share("d", wd, 1)
    pass_on(4)
    gather(0)
    experts(0, 3, 0, ROWS // 2)
    arrive(share_gate + share_up + share_down)
    experts(3, 4, 0, ROWS // 2)
    combine(0)

    sums = {}

    def send_sum(distance):
        way = -1 if distance > 0 else 1
        at = SLOT[distance]
        for half in range(2):
            part = pl.ds(half * (TOK // 2), TOK // 2)
            if distance in (4, -3):
                src = contrib.at[at, part]
            else:
                arrive(sums[distance - way, half])
                inbox = SLOT[distance - way]
                rs_out[at, part, :] = (
                    contrib[at, part, :].astype(F32) + rs_in[inbox, part, :].astype(F32)
                ).astype(BF)
                src = rs_out.at[at, part]
            sums[distance, half] = go([
                remote(f"s{distance}{half}", src, rs_in.at[at, part], along_z(way))
            ])

    send_sum(4)
    send_sum(-3)
    experts(2, 4, ROWS // 2, ROWS)
    combine(1)

    send_sum(3)
    send_sum(-2)
    send_sum(2)
    send_sum(-1)
    send_sum(1)
    for half in range(2):
        part = pl.ds(half * (TOK // 2), TOK // 2)
        arrive(sums[-1, half] + sums[1, half])
        mix_ref[part, :] = (
            contrib[SLOT[0], part, :].astype(F32)
            + rs_in[SLOT[1], part, :].astype(F32)
            + rs_in[SLOT[-1], part, :].astype(F32)
        ).astype(BF)
    for one in started:
        one.wait_send()


COPIES = 4 + 48 + 21 + 6 + 6 + 14


def on_device(
    q, k, v, strength, rate, factor, extra, s0, residual, seg, routes, gain, router, gate, up, down
):
    vmem = pl.BlockSpec(memory_space=pltpu.VMEM)
    hbm = pl.BlockSpec(memory_space=pl.ANY)
    V = pltpu.VMEM
    attended, ends, mixed = pl.pallas_call(
        kernel,
        out_shape=(
            jax.ShapeDtypeStruct((CHUNKS * C, C), F32),
            jax.ShapeDtypeStruct((1, 1, C, C), F32),
            jax.ShapeDtypeStruct((TOK, D), BF),
        ),
        in_specs=[vmem] * 13 + [hbm] * 3,
        out_specs=(vmem, vmem, vmem),
        scratch_shapes=[
            V((2, SHARDS, DEPTH, FE), BF),
            V((2, SHARDS, DEPTH, FE), BF),
            V((LOCAL, D, FE), BF),
            V((LOCAL, D, FE), BF),
            V((LOCAL, FE, D), BF),
            V((WINDOW, TOK, D), BF),
            V((WINDOW, EXPERTS, TOK), BF),
            V((WINDOW, 8, TOK), F32),
            V((WINDOW, 8, TOK), F32),
            V((LOCAL, WINDOW * CAP, D), BF),
            V((LOCAL, WINDOW * CAP, D), BF),
            V((WINDOW, TOK, D), BF),
            V((WINDOW, TOK, D), BF),
            V((WINDOW, TOK, D), BF),
            V((CHUNKS, 2 * C, C), BF),
            V((CHUNKS, C, C), F32),
            V((CHUNKS, C, C), F32),
            V((CHUNKS, C, C), F32),
            V((C, 2 * C), F32),
            V((SIDE, C, 2 * C), F32),
            V((SIDE, C, 2 * C), F32),
            V((C, C), F32),
            pltpu.SemaphoreType.DMA((COPIES,)),
            pltpu.SemaphoreType.DMA((COPIES,)),
            pltpu.SemaphoreType.DMA((4,)),
        ],
        compiler_params=pltpu.CompilerParams(
            collective_id=0, has_side_effects=True, vmem_limit_bytes=58 << 20
        ),
        cost_estimate=pl.CostEstimate(
            flops=7_000_000_000, bytes_accessed=6_000_000, transcendentals=2_000_000
        ),
    )(
        q, k, v,
        strength.reshape(CHUNKS, C), rate, factor.reshape(CHUNKS, C), extra.reshape(CHUNKS, C),
        s0, residual, seg.reshape(1, TOK), routes.T, gain, router.T, gate, up, down,
    )
    return attended.astype(BF), ends, mixed


def solution(mesh):
    placed = (
        P("ctx", "exp"), P("ctx", "exp"), P("ctx", "exp"), P("exp", "ctx"), P("exp", None),
        P("exp", "ctx"), P("exp", "ctx"), P("exp", None, None), P(("ctx", "exp"), None),
        P(("ctx", "exp")), P(("ctx", "exp"), None), P(), P(),
        P("exp", "ctx", None), P("exp", "ctx", None), P("exp", "ctx", None),
    )
    return jax.shard_map(
        on_device,
        mesh=mesh,
        in_specs=placed,
        out_specs=(P("ctx", "exp"), P("ctx", "exp", None, None), P(("ctx", "exp"), None)),
        check_vma=False,
    )
```

```python
import functools

import jax
import jax.numpy as jnp
from jax import lax
from jax.experimental import pallas as pl
from jax.experimental.pallas import tpu as pltpu
from jax.sharding import PartitionSpec as P

F32 = jnp.float32
BF = jnp.bfloat16
MESH = pl.DeviceIdType.MESH

C = 128
CHUNKS = 8
TOK = 128
CAP = 40
EXPERTS = 32
MODAL = 3
D = 1152
FE = 512
SIDE = 4
SHARDS = SIDE * SIDE
DEPTH = D // SHARDS
WIDTH = FE // SHARDS
WINDOW = 8
LOCAL = 4
route_scale = 2.446
norm_eps = 1e-06

SLOT = {4: 0, -3: 1, 3: 2, -2: 3, 2: 4, -1: 5, 1: 6, 0: 7}


def dn(a, b, ca, cb):
    return lax.dot_general(
        a.astype(BF), b.astype(BF), (((ca,), (cb,)), ((), ())), preferred_element_type=F32
    )


def split(a):
    high = a.astype(BF)
    return high, (a - high.astype(F32)).astype(BF)


def dot3(a, b):
    ah, al = split(a)
    bh, bl = split(b)
    return dn(ah, bh, 1, 0) + dn(ah, bl, 1, 0) + dn(al, bh, 1, 0)


def unit(v):
    return v * lax.rsqrt(jnp.sum(v * v, axis=-1, keepdims=True) + norm_eps)


def iotas(shape):
    return (
        lax.broadcasted_iota(jnp.int32, shape, 0),
        lax.broadcasted_iota(jnp.int32, shape, 1),
    )


def chunk_terms(n, q_ref, k_ref, v_ref, f_ref, x_ref, b_ref, rate_ref, readers, inner, added, decay):
    row, col = iotas((C, C))
    rows = pl.ds(pl.multiple_of(n * C, C), C)
    ku = unit(k_ref[rows, :].astype(F32))
    qu = unit(q_ref[rows, :].astype(F32))
    v = v_ref[rows, :].astype(F32)
    f = f_ref[pl.ds(n, 1), :]
    x = x_ref[pl.ds(n, 1), :]
    b = b_ref[pl.ds(n, 1), :]
    fc = jnp.sum(jnp.where(col <= row, f, 0.0), axis=1, keepdims=True)
    xc = jnp.sum(jnp.where(col <= row, x, 0.0), axis=1, keepdims=True)
    bc = jnp.sum(jnp.where(col == row, b, 0.0), axis=1, keepdims=True)
    cum = -(rate_ref[0:1, :] * fc + xc)
    last = cum[C - 1 : C, :]
    grown = jnp.exp(cum)
    kg = ku * grown
    ks = ku * jnp.exp(-cum)
    qg = qu * grown
    ke = ku * jnp.exp(last - cum)
    scores = dn(jnp.concatenate([kg, qg], 0), ks, 1, 1)
    a = jnp.where(col < row, scores[:C] * bc, 0.0)
    low = jnp.where(col <= row, scores[C:], 0.0)
    eye = jnp.where(col == row, 1.0, 0.0)
    inverse = eye - a
    square = dn(a, a, 1, 0)
    for level in range(6):
        if level < 5:
            r = dn(jnp.concatenate([inverse, square], 0), square, 1, 0)
            inverse = inverse + r[:C]
            square = r[C:]
        else:
            inverse = inverse + dn(inverse, square, 1, 0)
    solved = dn(inverse, jnp.concatenate([v * bc, kg * bc], 1), 1, 0)
    r1 = dn(low, solved, 1, 0)
    r2 = dn(ke, solved, 0, 0)
    inner[n] = r1[:, :C]
    readers[n] = jnp.concatenate([(qg - r1[:, C:]).astype(BF), r2[:, C:].astype(BF)], 0)
    added[n] = r2[:, :C]
    column = jnp.sum(jnp.where(col == row, jnp.exp(last), 0.0), axis=1, keepdims=True)
    decay[n] = jnp.broadcast_to(column, (C, C))


def kernel(
    q_hbm, k_hbm, v_hbm, b_ref, rate_ref, f_ref, x_ref, s0_hbm, res_hbm, seg_ref, routes_ref,
    gain_ref, router_ref, gate_ref, up_ref, down_ref,
    att_ref, state_ref, mix_ref,
    gs, us, wg, wu, wd, tok, table, slot_ids, slot_w, xin, eo, contrib, rs_out,
    rs_in, readers, inner, added, decay, gmap, rowmaps, colmaps, state,
    q_ref, k_ref, v_ref, s0_ref, res_ref, send_sem, recv_sem, loc_sem,
):
    ctx = lax.axis_index("ctx")
    own = lax.axis_index("exp")
    px, py = ctx // SIDE, ctx % SIDE
    pz, core = own // 2, own % 2
    planes = EXPERTS // 2
    sense = 1 - 2 * core

    def along_z(steps):
        return (ctx, lax.rem(pz + sense * steps + planes, planes) * 2 + core)

    def along_x(steps):
        return (lax.rem(px + sense * steps + SIDE, SIDE) * SIDE + py, own)

    def along_y(steps):
        return (px * SIDE + lax.rem(py + sense * steps + SIDE, SIDE), own)

    def along_column(steps):
        return (lax.rem(px + steps, SIDE) * SIDE + py, own)

    def along_row(steps):
        return (px * SIDE + lax.rem(py + steps, SIDE), own)

    sibling = (ctx, pz * 2 + 1 - core)
    ids = {}

    def remote(name, src, dst, device):
        k = ids.setdefault(name, len(ids))
        return pltpu.make_async_remote_copy(
            src_ref=src, dst_ref=dst, send_sem=send_sem.at[k], recv_sem=recv_sem.at[k],
            device_id=device, device_id_type=MESH,
        )

    started = []

    def go(copies):
        for one in copies:
            one.start()
        started.extend(copies)
        return copies

    def arrive(copies):
        for one in copies:
            one.wait_recv()

    reads = [
        pltpu.make_async_copy(src, dst, loc_sem.at[4 + n])
        for n, (src, dst) in enumerate((
            (res_hbm, res_ref), (q_hbm, q_ref), (k_hbm, k_ref), (v_hbm, v_ref), (s0_hbm, s0_ref),
        ))
    ]
    for one in reads:
        one.start()

    barrier = pltpu.get_barrier_semaphore()
    partners = [along_z(t) for t in (1, -1, 8)] + [sibling]
    partners += [along_column(t) for t in (1, 2, 3)] + [along_row(t) for t in (1, 2, 3)]
    for device in partners:
        pl.semaphore_signal(barrier, inc=1, device_id=device, device_id_type=MESH)
    pl.semaphore_wait(barrier, len(partners))

    HALF = FE // 2
    pieces = {}
    for r in range(2):
        pieces["g", r] = (
            lambda i, r=r: gs.at[r, i],
            lambda i, r=r: gs.at[r, pl.ds(i * SIDE, SIDE)],
            gate_ref.at[0], True,
        )
        for half in range(2):
            cols = pl.ds(half * HALF, HALF)
            pieces[f"u{half}", r] = (
                lambda i, r=r, cols=cols: us.at[r, i, :, cols],
                lambda i, r=r, cols=cols: us.at[r, pl.ds(i * SIDE, SIDE), :, cols],
                up_ref.at[0, :, cols], half == 0,
            )
        pieces["d", r] = (
            lambda i, r=r: wd.at[2 * r, pl.ds(pl.multiple_of(i * WIDTH, WIDTH), WIDTH)],
            lambda i, r=r: wd.at[
                2 * r, pl.ds(pl.multiple_of(i * SIDE * WIDTH, SIDE * WIDTH), SIDE * WIDTH)
            ],
            down_ref.at[0], False,
        )
    moves = {}

    def place(key):
        x_first = pieces[key][3]
        return (px, py, along_x, along_y) if x_first else (py, px, along_y, along_x)

    def near(key):
        one, block, given, x_first = pieces[key]
        a, b, axis, other = place(key)
        here = one(b * SIDE + a)
        src = given if key[1] == 0 else here
        moves[key] = [
            remote(f"{key}p", src, here, axis(1)), remote(f"{key}m", src, here, axis(-1))
        ]
        go(moves[key])

    def near_on(key):
        one, block, given, x_first = pieces[key]
        a, b, axis, other = place(key)
        arrive(moves[key][:1])
        from_behind = one(b * SIDE + lax.rem(a - sense + SIDE, SIDE))
        moves[key].append(remote(f"{key}f", from_behind, from_behind, axis(1)))
        go(moves[key][2:])

    def far(key):
        one, block, given, x_first = pieces[key]
        a, b, axis, other = place(key)
        arrive(moves[key][1:])
        line = block(b)
        moves[key] = [
            remote(f"{key}P", line, line, other(1)), remote(f"{key}M", line, line, other(-1))
        ]
        go(moves[key])

    def far_on(key):
        one, block, given, x_first = pieces[key]
        a, b, axis, other = place(key)
        arrive(moves[key][:1])
        line = block(lax.rem(b - sense + SIDE, SIDE))
        moves[key].append(remote(f"{key}F", line, line, other(1)))
        go(moves[key][2:])

    def complete(key):
        arrive(moves[key][1:])

    KINDS = ("g", "u0", "u1", "d")
    across = {}
    locals_ = []

    def cross(kind):
        one, block, given, x_first = pieces[kind, 1]
        a, b, axis, other = place((kind, 1))
        across[kind] = go([remote(f"{kind}z", given, one(b * SIDE + a), along_z(8))])

    for kind in KINDS:
        cross(kind)
    for n, kind in enumerate(KINDS):
        one, block, given, x_first = pieces[kind, 0]
        a, b, axis, other = place((kind, 0))
        near((kind, 0))
        locals_.append(pltpu.make_async_copy(given, one(b * SIDE + a), loc_sem.at[n]))
        locals_[-1].start()

    def each(step, r, kinds=KINDS):
        for kind in kinds:
            step((kind, r))

    def crossed_one(key):
        arrive(across[key[0]])
        near(key)

    for one in reads:
        one.wait()
    row, col = iotas((C, C))
    stream = res_ref[...].astype(F32)
    scale = lax.rsqrt(jnp.mean(stream * stream, axis=1, keepdims=True) + norm_eps)
    seg = seg_ref[...].astype(F32)
    modality = seg - MODAL * jnp.floor((seg + 0.5) * (1.0 / MODAL))
    modality = jnp.sum(jnp.where(col == row, modality, 0.0), axis=1, keepdims=True)
    gains = jnp.where(
        modality == 0.0,
        gain_ref[0:1, :],
        jnp.where(modality == 1.0, gain_ref[1:2, :], gain_ref[2:3, :]),
    )
    normed = (stream * scale * gains).astype(BF)
    tok[SLOT[0]] = normed
    logits = dn(router_ref[...], normed, 1, 1)
    expert = lax.broadcasted_iota(jnp.int32, (EXPERTS, TOK), 0)
    hits = jnp.zeros((EXPERTS, TOK), F32)
    for turn in range(8):
        hits = hits + jnp.where(routes_ref[turn : turn + 1, :] == expert, 1.0, 0.0)
    scores = jnp.where(hits > 0.0, 1.0 / (1.0 + jnp.exp(-logits)), 0.0)
    weights = route_scale * scores / jnp.sum(scores, axis=0, keepdims=True)
    table[SLOT[0]] = weights.astype(BF)

    def token_step(way, k, half):
        src, dst = SLOT[way * (k - 1)], SLOT[way * k]
        part = pl.ds(half * (TOK // 2), TOK // 2)
        copies = []
        if half == 0:
            copies.append(remote(f"w{way}{k}", table.at[src], table.at[dst], along_z(way)))
        copies.append(
            remote(f"t{way}{k}{half}", tok.at[src, part], tok.at[dst, part], along_z(way))
        )
        return go(copies)

    hops = {}

    def first_hop():
        for half in range(2):
            for way in (1, -1):
                hops[way, 1, half] = token_step(way, 1, half)

    def pass_on(k):
        for half in range(2):
            for way, last in ((1, 4), (-1, 3)):
                if k <= last:
                    arrive(hops[way, k, half])
                if k < last:
                    hops[way, k + 1, half] = token_step(way, k + 1, half)

    def chunks(lo, hi):
        def body(n, carry):
            chunk_terms(
                n, q_ref, k_ref, v_ref, f_ref, x_ref, b_ref, rate_ref, readers, inner, added, decay
            )
            return carry

        lax.fori_loop(lo, hi, body, 0)

    def merge(src, r, dst, kinds):
        def body(h, carry):
            at = pl.ds(pl.multiple_of(h * 2 * DEPTH, 2 * DEPTH), 2 * DEPTH)
            for lo, hi, x_first in kinds:
                parts = []
                for late in range(2):
                    i = 2 * h + late
                    where = (i % SIDE) * SIDE + i // SIDE if x_first else i
                    parts.append(src[r, where, :, lo:hi].astype(F32))
                dst[2 * r, at, lo:hi] = jnp.concatenate(parts, 0).astype(BF)
            return carry

        lax.fori_loop(0, SHARDS // 2, body, 0)

    GATE_KINDS = [(0, FE, True)]
    UP_KINDS = [(0, HALF, True), (HALF, FE, False)]

    def share(kind, held, r):
        return go([remote(f"s{kind}{r}", held.at[2 * r], held.at[2 * r + 1], sibling)])

    def outputs(n, carry):
        s = state[...]
        r = dn(readers[n], s, 1, 0)
        att_ref[pl.ds(pl.multiple_of(n * C, C), C), :] = inner[n] + r[:C]
        state[...] = decay[n] * s - r[C:] + added[n]
        return carry

    upper = jnp.where(row <= col, 1.0, 0.0)
    pick_row, pick_col = iotas((8, EXPERTS))
    mine = []
    for r in range(2):
        plane = lax.rem(pz + 8 * r, planes)
        mine += [2 * plane + core, 2 * plane + 1 - core]
    select = jnp.zeros((8, EXPERTS), F32)
    for e in range(LOCAL):
        select = select + jnp.where((pick_row == e) & (pick_col == mine[e]), 1.0, 0.0)

    PAIR = 2 * CAP
    place_rows = lax.broadcasted_iota(jnp.int32, (PAIR, 2 * TOK), 0).astype(F32)

    def spread(pair, weighted):
        a, b = 2 * pair, 2 * pair + 1
        parts = []
        for e in range(LOCAL):
            ids_row = jnp.concatenate([slot_ids[a, e : e + 1, :], slot_ids[b, e : e + 1, :]], 1)
            if weighted:
                value = jnp.concatenate([slot_w[a, e : e + 1, :], slot_w[b, e : e + 1, :]], 1)
            else:
                value = 1.0
            parts.append(jnp.where(place_rows == ids_row, value, 0.0))
        return jnp.concatenate(parts, 0).astype(BF)

    def gather(group):
        for half in range(2):
            pair = 2 * group + half
            for slot in (2 * pair, 2 * pair + 1):
                w = dn(select, table[slot], 1, 0)
                hit = w != 0.0
                count = dn(jnp.where(hit, 1.0, 0.0), upper, 1, 0)
                slot_ids[slot] = jnp.where(hit, count + (CAP * (slot % 2) - 1.0), -1.0)
                slot_w[slot] = w
            both = tok[2 * pair : 2 * pair + 2].reshape(2 * TOK, D)
            rows = dn(spread(pair, False), both, 1, 0).astype(BF)
            for e in range(LOCAL):
                xin[e, pair * PAIR : (pair + 1) * PAIR, :] = rows[e * PAIR : (e + 1) * PAIR]

    def experts(lo, hi, first, last):
        def body(e, carry):
            x = xin[e, first:last, :]
            g = dn(x, wg[e], 1, 0)
            u = dn(x, wu[e], 1, 0)
            hidden = (g / (1.0 + jnp.exp(-g)) * u).astype(BF)
            eo[e, first:last, :] = dn(hidden, wd[e], 1, 0).astype(BF)
            return carry

        if hi - lo == 1:
            body(lo, 0)
        else:
            lax.fori_loop(lo, hi, body, 0)

    def combine(group):
        for half in range(2):
            pair = 2 * group + half
            made = jnp.concatenate(
                [eo[e, pair * PAIR : (pair + 1) * PAIR, :] for e in range(LOCAL)], 0
            )
            both = dn(spread(pair, True), made, 0, 0)
            contrib[2 * pair] = both[:TOK].astype(BF)
            contrib[2 * pair + 1] = both[TOK:].astype(BF)

    each(near_on, 0)
    chunks(0, 2)
    for one in locals_:
        one.wait()
    each(far, 0)
    chunks(2, 8)
    gmap[...] = jnp.concatenate([jnp.zeros((C, C), F32), jnp.where(col == row, 1.0, 0.0)], 1)

    def grow(n, carry):
        d = decay[n]
        m = gmap[...]
        r = dn(readers[n, C:], m, 1, 0)
        gmap[...] = jnp.concatenate(
            [d * m[:, :C] - r[:, :C] + added[n], d * m[:, C:] - r[:, C:]], 1
        )
        return carry

    lax.fori_loop(0, CHUNKS, grow, 0)
    rowmaps[py] = gmap[...]
    row_copies = go([
        remote(f"r{t}", gmap, rowmaps.at[py], along_row(t)) for t in (1, 3, 2)
    ])
    each(far_on, 0)
    each(crossed_one, 1)
    first_hop()
    arrive(row_copies)
    whole = rowmaps[0]
    for t in range(1, SIDE):
        m = rowmaps[t]
        whole = dot3(m[:, C:], whole)
        whole = jnp.concatenate([whole[:, :C] + m[:, :C], whole[:, C:]], 1)
    colmaps[px] = whole
    col_copies = go([
        remote(f"c{t}", colmaps.at[px], colmaps.at[px], along_column(t)) for t in (1, 3, 2)
    ])
    each(near_on, 1)
    each(far, 1)
    pass_on(1)
    each(complete, 0)
    merge(gs, 0, wg, GATE_KINDS)
    merge(us, 0, wu, UP_KINDS)
    share_own = share("g", wg, 0) + share("u", wu, 0) + share("d", wd, 0)
    arrive(col_copies)
    entering = s0_ref[0]
    for t in range(SIDE - 1):
        m = colmaps[t]
        entering = jnp.where(px > t, dot3(m[:, C:], entering) + m[:, :C], entering)
    for t in range(SIDE - 1):
        m = rowmaps[t]
        entering = jnp.where(py > t, dot3(m[:, C:], entering) + m[:, :C], entering)
    state[...] = entering
    pass_on(2)
    each(far_on, 1)
    gather(1)
    arrive(share_own)
    ROWS = WINDOW * CAP
    experts(0, 2, ROWS // 2, ROWS)
    pass_on(3)
    lax.fori_loop(0, CHUNKS, outputs, 0)
    state_ref[0, 0] = state[...]
    complete(("g", 1))
    merge(gs, 1, wg, GATE_KINDS)
    share_gate = share("g", wg, 1)
    complete(("u0", 1))
    complete(("u1", 1))
    merge(us, 1, wu, UP_KINDS)
    share_up = share("u", wu, 1)
    complete(("d", 1))
    share_down = share("d", wd, 1)
    pass_on(4)
    gather(0)
    experts(0, 3, 0, ROWS // 2)
    arrive(share_gate + share_up + share_down)
    experts(3, 4, 0, ROWS // 2)
    combine(0)

    sums = {}

    def send_sum(distance):
        way = -1 if distance > 0 else 1
        at = SLOT[distance]
        for half in range(2):
            part = pl.ds(half * (TOK // 2), TOK // 2)
            if distance in (4, -3):
                src = contrib.at[at, part]
            else:
                arrive(sums[distance - way, half])
                inbox = SLOT[distance - way]
                rs_out[at, part, :] = (
                    contrib[at, part, :].astype(F32) + rs_in[inbox, part, :].astype(F32)
                ).astype(BF)
                src = rs_out.at[at, part]
            sums[distance, half] = go([
                remote(f"s{distance}{half}", src, rs_in.at[at, part], along_z(way))
            ])

    send_sum(4)
    send_sum(-3)
    experts(2, 4, ROWS // 2, ROWS)
    combine(1)

    send_sum(3)
    send_sum(-2)
    send_sum(2)
    send_sum(-1)
    send_sum(1)
    for half in range(2):
        part = pl.ds(half * (TOK // 2), TOK // 2)
        arrive(sums[-1, half] + sums[1, half])
        mix_ref[part, :] = (
            contrib[SLOT[0], part, :].astype(F32)
            + rs_in[SLOT[1], part, :].astype(F32)
            + rs_in[SLOT[-1], part, :].astype(F32)
        ).astype(BF)
    for one in started:
        one.wait_send()


COPIES = 4 + 48 + 21 + 6 + 6 + 14


def on_device(
    q, k, v, strength, rate, factor, extra, s0, residual, seg, routes, gain, router, gate, up, down
):
    vmem = pl.BlockSpec(memory_space=pltpu.VMEM)
    hbm = pl.BlockSpec(memory_space=pl.ANY)
    V = pltpu.VMEM
    attended, ends, mixed = pl.pallas_call(
        kernel,
        out_shape=(
            jax.ShapeDtypeStruct((CHUNKS * C, C), F32),
            jax.ShapeDtypeStruct((1, 1, C, C), F32),
            jax.ShapeDtypeStruct((TOK, D), BF),
        ),
        in_specs=[hbm] * 3 + [vmem] * 4 + [hbm] * 2 + [vmem] * 4 + [hbm] * 3,
        out_specs=(vmem, vmem, vmem),
        scratch_shapes=[
            V((2, SHARDS, DEPTH, FE), BF),
            V((2, SHARDS, DEPTH, FE), BF),
            V((LOCAL, D, FE), BF),
            V((LOCAL, D, FE), BF),
            V((LOCAL, FE, D), BF),
            V((WINDOW, TOK, D), BF),
            V((WINDOW, EXPERTS, TOK), BF),
            V((WINDOW, 8, TOK), F32),
            V((WINDOW, 8, TOK), F32),
            V((LOCAL, WINDOW * CAP, D), BF),
            V((LOCAL, WINDOW * CAP, D), BF),
            V((WINDOW, TOK, D), BF),
            V((WINDOW, TOK, D), BF),
            V((WINDOW, TOK, D), BF),
            V((CHUNKS, 2 * C, C), BF),
            V((CHUNKS, C, C), F32),
            V((CHUNKS, C, C), F32),
            V((CHUNKS, C, C), F32),
            V((C, 2 * C), F32),
            V((SIDE, C, 2 * C), F32),
            V((SIDE, C, 2 * C), F32),
            V((C, C), F32),
            V((CHUNKS * C, C), BF),
            V((CHUNKS * C, C), BF),
            V((CHUNKS * C, C), BF),
            V((1, C, C), F32),
            V((TOK, D), BF),
            pltpu.SemaphoreType.DMA((COPIES,)),
            pltpu.SemaphoreType.DMA((COPIES,)),
            pltpu.SemaphoreType.DMA((9,)),
        ],
        compiler_params=pltpu.CompilerParams(
            collective_id=0, has_side_effects=True, vmem_limit_bytes=58 << 20
        ),
        cost_estimate=pl.CostEstimate(
            flops=7_000_000_000, bytes_accessed=6_000_000, transcendentals=2_000_000
        ),
    )(
        q, k, v,
        strength.reshape(CHUNKS, C), rate, factor.reshape(CHUNKS, C), extra.reshape(CHUNKS, C),
        s0, residual, seg.reshape(1, TOK), routes.T, gain, router.T, gate, up, down,
    )
    return attended.astype(BF), ends, mixed


def solution(mesh):
    placed = (
        P("ctx", "exp"), P("ctx", "exp"), P("ctx", "exp"), P("exp", "ctx"), P("exp", None),
        P("exp", "ctx"), P("exp", "ctx"), P("exp", None, None), P(("ctx", "exp"), None),
        P(("ctx", "exp")), P(("ctx", "exp"), None), P(), P(),
        P("exp", "ctx", None), P("exp", "ctx", None), P("exp", "ctx", None),
    )
    return jax.shard_map(
        on_device,
        mesh=mesh,
        in_specs=placed,
        out_specs=(P("ctx", "exp"), P("ctx", "exp", None, None), P(("ctx", "exp"), None)),
        check_vma=False,
    )
```
